512 devices in a mesh: lon: 32 (over x, y, z_hi), lat: 16 (over z_lo, core).
Axes of the slice: x: 4, y: 4, z: 16 (z_hi: 2, z_lo: 8; z = z_hi * 8 + z_lo), core: 2. Of those that a mesh axis runs over, the one named last changes fastest.
Arguments:
- tracer: float32 [4, 1, 2048, 4096], P(None, None, 'lat', 'lon'), may hold values from -6 to 6
- final_adjoint: float32 [4, 1, 2048, 4096], P(None, None, 'lat', 'lon'), may hold values from -6 to 6
- speed_east: float32 [1, 2048, 4096], P(None, 'lat', 'lon'), may hold values from 0.1 to 1
- speed_north: float32 [1, 2048, 4096], P(None, 'lat', 'lon'), may hold values from 0.1 to 1
- sign_east: int32 [1, 2048, 4096], P(None, 'lat', 'lon'), may hold values 0 or 1
- sign_north: int32 [1, 2048, 4096], P(None, 'lat', 'lon'), may hold values 0 or 1
- density: float32 [1, 2048, 4096], P(None, 'lat', 'lon'), may hold values from 0.6 to 1.5
- land_type: int32 [2048, 4096], P('lat', 'lon'), may hold values from 0 to 7
- source_mask: int32 [2048, 4096], P('lat', 'lon'), may hold values 0 or 1
- emission: float32 [4, 2048, 4096], P(None, 'lat', 'lon'), may hold values from 0.2 to 2
- deposition: float32 [8, 4], replicated, may hold values from 0.2 to 2
Outputs:
- adjoint_tracer: float32 [4, 1, 2048, 4096], P(None, None, 'lat', 'lon')
- density_grad: float32 [1, 2048, 4096], P(None, 'lat', 'lon')
- emission_grad: float32 [4, 2048, 4096], P(None, 'lat', 'lon')
The draws below stay inside these ranges and needn't reach their ends.
Inputs may be any that keep to these rules, and one draw needn't show every extreme that they name: `sign_east`: 1 where the western face's wind blows toward higher longitude index, 0 where it blows the other way. `sign_north`: 1 where the southern face's wind blows toward higher latitude index, 0 where it blows the other way.
All inputs are finite; a program needn't handle non-finite values. No bound on the sum of `sign_east` or of `sign_north` or of `source_mask` on one device may be relied on, other than what follows from the above.
Results may differ from the reference program's by a relative error of at most 0.0003.
Values sent between devices are 32-bit elements; how exact they have to be, the bound alone decides.
No kernel may reach another device: no remote copies, remote signals or barrier semaphores. Data moves between devices by JAX's collectives and lax.ppermute only.
A program may use at most 64 MiB of HBM per device.

```python
import math
import jax
import jax.numpy as jnp
from jax import lax

BINS = 4
LANDS = 8
LEV = 1
NLAT = 2048
NLON = 4096


def set_ends(array, rng, least, top_value):
    longest = array.shape.index(max(array.shape))
    spots = []
    for shift in (0, 1):
        where = [jax.random.randint(jax.random.fold_in(rng, axis), (), 0, length) for axis, length in enumerate(array.shape)]
        where[longest] = (where[longest] + shift) % array.shape[longest]
        spots.append(tuple(where))
    return array.at[spots[0]].set(least).at[spots[1]].set(top_value)


def level_of(key, shape, cuts, smallest, top_value):
    def one(axis_at, blocks):
        steps = jax.random.uniform(jax.random.fold_in(jax.random.fold_in(key, 6), axis_at), (blocks,), jnp.float32, smallest / len(cuts), top_value / len(cuts))
        return jnp.repeat(jnp.exp(steps), shape[axis_at] // blocks).reshape((-1,) + (1,) * (len(shape) - axis_at - 1))

    gain = one(*cuts[0])
    for cut in cuts[1:]:
        gain = gain * one(*cut)
    return gain


def bell_draw(stream_key, shape, scale, bound, split=(), dtype=jnp.bfloat16):
    drawn = scale * jax.random.normal(stream_key, shape, jnp.float32)
    if split:
        drawn = drawn * level_of(stream_key, shape, split, -0.22, 0.18)
    return jnp.clip(drawn, -bound, bound).astype(dtype)


def setup_inputs(seed: int = 0) -> dict:
    key_of = jax.random.split(jax.random.key(seed), 12)
    return {
        "tracer": bell_draw(key_of[0], (BINS, LEV, NLAT, NLON), 1.0, 6.0, ((2, 16), (3, 32)), jnp.float32),
        "final_adjoint": bell_draw(key_of[1], (BINS, LEV, NLAT, NLON), 1.0, 6.0, ((2, 16), (3, 32)), jnp.float32),
        "speed_east": jnp.clip(jnp.exp(math.log(1.0) - 2.3025851 * jax.random.uniform(key_of[2], (LEV, NLAT, NLON), jnp.float32) ** level_of(key_of[2], (LEV, NLAT, NLON), ((1, 16), (2, 32)), -0.2, 0.2)), 0.1, 1.0),
        "speed_north": jnp.clip(jnp.exp(math.log(1.0) - 2.3025851 * jax.random.uniform(key_of[3], (LEV, NLAT, NLON), jnp.float32) ** level_of(key_of[3], (LEV, NLAT, NLON), ((1, 16), (2, 32)), -0.2, 0.2)), 0.1, 1.0),
        "sign_east": set_ends((jax.random.randint(key_of[4], (LEV, NLAT, NLON), 0, 2) < 1).astype(jnp.int32), jax.random.fold_in(key_of[4], 1), 0, 1),
        "sign_north": set_ends((jax.random.randint(key_of[5], (LEV, NLAT, NLON), 0, 2) < 1).astype(jnp.int32), jax.random.fold_in(key_of[5], 1), 0, 1),
        "density": jnp.clip(0.6 + 0.9 * jax.random.uniform(key_of[6], (LEV, NLAT, NLON), jnp.float32) ** level_of(key_of[6], (LEV, NLAT, NLON), ((1, 16), (2, 32)), -0.2, 0.2), 0.6, 1.5),
        "land_type": set_ends(jax.random.randint(key_of[7], (NLAT, NLON), 0, LANDS), jax.random.fold_in(key_of[7], 1), 0, LANDS - 1).astype(jnp.int32),
        "source_mask": set_ends((jax.random.randint(key_of[8], (NLAT, NLON), 0, 3) < 1).astype(jnp.int32), jax.random.fold_in(key_of[8], 1), 0, 1),
        "emission": jnp.clip(jnp.exp(math.log(2.0) - 2.3025851 * jax.random.uniform(key_of[9], (BINS, NLAT, NLON), jnp.float32) ** level_of(key_of[9], (BINS, NLAT, NLON), ((1, 16), (2, 32)), -0.2, 0.2)), 0.2, 2.0),
        "deposition": jnp.clip(jnp.exp(jax.random.uniform(key_of[10], (LANDS, BINS), jnp.float32, math.log(0.2), math.log(2.0))), 0.2, 2.0),
    }


COURANT = 0.3
TIME_STEP = 0.25

def lon_cut(values, begin_at, end_at):
    return values[..., begin_at:end_at]

def lat_cut(values, begin_at, end_at):
    return values[..., begin_at:end_at, :]

def divergence(tracer, velocity, density, cutter, extent):
    far_back = cutter(tracer, 0, extent - 3)
    behind = cutter(tracer, 1, extent - 2)
    center = cutter(tracer, 2, extent - 1)
    in_front = cutter(tracer, 3, extent)
    from_back = (-far_back + 5.0 * behind + 2.0 * center) / 6.0
    from_front = (2.0 * behind + 5.0 * center - in_front) / 6.0
    signed_wind = cutter(velocity, 2, extent - 1)
    face_mass = signed_wind * (0.5 * (cutter(density, 1, extent - 2) + cutter(density, 2, extent - 1)))
    fluxes = face_mass * jnp.where(signed_wind > 0.0, from_back, from_front)
    return cutter(fluxes, 1, extent - 3) - cutter(fluxes, 0, extent - 4)

def advance(tracer, wind_east, wind_north, density, losses, source, weight):
    row_count = tracer.shape[-2]
    col_count = tracer.shape[-1]
    east_change = divergence(tracer[..., 2:-2, :], wind_east[..., 2:-2, :], density[..., 2:-2, :], lon_cut, col_count)
    north_change = divergence(tracer[..., :, 2:-2], wind_north[..., :, 2:-2], density[..., :, 2:-2], lat_cut, row_count)
    interior = tracer[..., 2:-2, 2:-2]
    carried = interior - COURANT * (east_change + north_change) / density[..., 2:-2, 2:-2]
    surface = carried[:, 0] - losses[..., 2:-2, 2:-2] * weight * interior[:, 0] + source[..., 2:-2, 2:-2] * weight
    return jnp.concatenate([surface[:, None], carried[:, 1:]], axis=1)

def land_losses(land_type, deposition):
    land_kinds = deposition.shape[0]
    one_hot = (land_type[None] == lax.broadcasted_iota(jnp.int32, (land_kinds, 1, 1), 0)).astype(jnp.float32)
    return TIME_STEP * jnp.einsum('kb,krc->brc', deposition, one_hot, precision=lax.Precision.HIGHEST)

def pad_field(field, fill):
    wrapped = jnp.concatenate([field[..., -2:], field, field[..., :2]], axis=-1)
    widths = [(0, 0)] * (field.ndim - 2) + [(2, 2), (0, 0)]
    return jnp.pad(wrapped, widths, constant_values=fill)

def reference(tracer, final_adjoint, speed_east, speed_north, sign_east, sign_north, density, land_type, source_mask, emission, deposition):
    levels = tracer.shape[1]
    row_ids = lax.broadcasted_iota(jnp.int32, (tracer.shape[2], 1), 0)
    wind_east = jnp.where(sign_east == 1, speed_east, -speed_east)
    wind_north = jnp.where(row_ids == 0, 0.0, jnp.where(sign_north == 1, speed_north, -speed_north))
    losses = land_losses(land_type, deposition)
    source = TIME_STEP * source_mask.astype(jnp.float32) * emission
    losses_padded = pad_field(losses, 0.0)
    east_padded = pad_field(wind_east, 0.0)
    north_padded = pad_field(wind_north, 0.0)

    def level_pass(inputs):
        level_tracer, level_adjoint, level_east, level_north, level_density, weight = inputs

        def both_steps(start_tracer, step_density, step_source):
            density_padded = pad_field(step_density, 1.0)[None]
            source_padded = pad_field(step_source, 0.0)
            middle = advance(pad_field(start_tracer, 0.0)[:, None], level_east[None], level_north[None], density_padded, losses_padded, source_padded, weight)
            final = advance(pad_field(middle[:, 0], 0.0)[:, None], level_east[None], level_north[None], density_padded, losses_padded, source_padded, weight)
            return final[:, 0]
        unused_final, pullback = jax.vjp(both_steps, level_tracer, level_density, source)
        return pullback(level_adjoint)
    weights = (lax.broadcasted_iota(jnp.int32, (levels,), 0) == 0).astype(jnp.float32)
    inputs = (jnp.moveaxis(tracer, 1, 0), jnp.moveaxis(final_adjoint, 1, 0), east_padded, north_padded, density, weights)
    tracer_parts, density_grad, source_parts = lax.map(level_pass, inputs)
    adjoint_tracer = jnp.moveaxis(tracer_parts, 0, 1)
    source_grad = lax.optimization_barrier(jnp.sum(source_parts, axis=0))
    emission_grad = TIME_STEP * source_mask.astype(jnp.float32) * source_grad
    return (adjoint_tracer, density_grad, emission_grad)
```

```python
import functools

import jax
import jax.numpy as jnp
from jax import lax
from jax.experimental import pallas as pl
from jax.experimental.pallas import tpu as pltpu
from jax.sharding import PartitionSpec as P

COURANT = 0.3
TIME_STEP = 0.25

N = 128
BINS = 4
MAIN = 2 * BINS + 3
EXTRA = BINS + 1
EAST, NORTH, RHO = 2 * BINS, 2 * BINS + 1, 2 * BINS + 2
LINES = 4 * MAIN + 2 * EXTRA
LAT_MSG = 56
LON_MSG = 64
BASE = 16
ROWS = 160
F32 = jnp.float32


def plane_readers(refs, info):
    tracer, adjoint, speed_e, speed_n, sign_e, sign_n, density, land, mask, emission = refs

    def east(at, size):
        s = speed_e[0, pl.ds(at, size), :]
        return jnp.where(sign_e[0, pl.ds(at, size), :] == 1, s, -s)

    def north(at, size):
        s = speed_n[0, pl.ds(at, size), :]
        s = jnp.where(sign_n[0, pl.ds(at, size), :] == 1, s, -s)
        row = lax.broadcasted_iota(jnp.int32, (size, N), 0) + at
        return jnp.where((row == 0) & (info[2] == 1), 0.0, s)

    def source(b):
        def read(at, size):
            m = mask[pl.ds(at, size), :].astype(F32)
            return TIME_STEP * m * emission[b, pl.ds(at, size), :]

        return read

    main = [lambda at, size, b=b: tracer[b, 0, pl.ds(at, size), :] for b in range(BINS)]
    main += [lambda at, size, b=b: adjoint[b, 0, pl.ds(at, size), :] for b in range(BINS)]
    main += [east, north, lambda at, size: density[0, pl.ds(at, size), :]]
    extra = [source(b) for b in range(BINS)]
    extra += [lambda at, size: land[pl.ds(at, size), :].astype(F32)]
    return main, extra


def pack_kernel(info, *refs):
    ins, (out0, out1, lines_out), (edge, packed) = refs[:10], refs[10:13], refs[13:]
    main, extra = plane_readers(ins, info)
    lane = lax.broadcasted_iota(jnp.int32, (N, N), 1)
    for p, read in enumerate(main):
        edge[0, 4 * p : 4 * p + 4, :] = read(0, 8)[:4]
        edge[1, 4 * p : 4 * p + 4, :] = read(N - 8, 8)[4:]
    for q, read in enumerate(extra):
        at = 4 * MAIN + 2 * q
        edge[0, at : at + 2, :] = read(0, 8)[:2]
        edge[1, at : at + 2, :] = read(N - 8, 8)[6:]
    edge[:, LINES:LAT_MSG, :] = jnp.zeros((2, LAT_MSG - LINES, N), F32)
    parity = info[0]
    out0[...] = edge[1 - parity]
    out1[...] = edge[parity]
    both = jnp.zeros((N, N), F32)
    for p, read in enumerate(main):
        turned = pltpu.roll(read(0, N), 8 * p + 4, 1)
        both = jnp.where((lane >= 8 * p) & (lane < 8 * p + 8), turned, both)
    for q, read in enumerate(extra):
        at = 8 * MAIN + 4 * q
        turned = pltpu.roll(read(0, N), at + 2, 1)
        both = jnp.where((lane >= at) & (lane < at + 4), turned, both)
    packed[...] = both.T
    for p in range(MAIN):
        lines_out[1, 4 * p : 4 * p + 4, :] = packed[8 * p : 8 * p + 4, :]
        lines_out[0, 4 * p : 4 * p + 4, :] = packed[8 * p + 4 : 8 * p + 8, :]
    for q in range(EXTRA):
        at, to = 8 * MAIN + 4 * q, 4 * MAIN + 2 * q
        lines_out[1, to : to + 2, :] = packed[at : at + 2, :]
        lines_out[0, to : to + 2, :] = packed[at + 2 : at + 4, :]
    lines_out[:, LINES:LON_MSG, :] = jnp.zeros((2, LON_MSG - LINES, N), F32)


def place_lat(info, got0, got1, halo):
    parity = info[0]
    halo[1 - parity] = got0[...]
    halo[parity] = got1[...]
    at = 4 * RHO

    @pl.when(info[2] == 1)
    def _():
        halo[0, at : at + 4, :] = jnp.ones((4, N), F32)

    @pl.when(info[3] == 1)
    def _():
        halo[1, at : at + 4, :] = jnp.ones((4, N), F32)


def corner_kernel(info, got0, got1, lines, out, halo, rows):
    place_lat(info, got0, got1, halo)
    rows[8 * MAIN :, :] = jnp.zeros((N - 8 * MAIN, N), F32)
    for p in range(MAIN):
        rows[8 * p : 8 * p + 4, :] = halo[0, 4 * p : 4 * p + 4, :]
        rows[8 * p + 4 : 8 * p + 8, :] = halo[1, 4 * p : 4 * p + 4, :]
    turned = rows[...].T
    parity = info[1]
    out[0:LON_MSG, :] = lines[1 - parity]
    out[LON_MSG:, :] = lines[parity]
    left, right = turned[0:8][:4], turned[N - 8 :][4:]

    @pl.when(parity == 0)
    def _():
        out[LINES : LINES + 4, :] = right
        out[LON_MSG + LINES : LON_MSG + LINES + 4, :] = left

    @pl.when(parity == 1)
    def _():
        out[LINES : LINES + 4, :] = left
        out[LON_MSG + LINES : LON_MSG + LINES + 4, :] = right


def main_kernel(info, deposition, *refs):
    ins = refs[:10]
    got0, got1, near, passed = refs[10:14]
    adj_out, dens_out, emis_out = refs[14:17]
    (halo, sides, turn, main, extra, mass, inv, keep, g, middle, second, flux, back, flux2, bank, hn, dens) = refs[17:]
    read_main, read_extra = plane_readers(ins, info)
    lane = lax.broadcasted_iota(jnp.int32, (8, N), 1)

    place_lat(info, got0, got1, halo)
    parity = info[1]
    sides[1 - parity] = near[0:LON_MSG, :]
    sides[parity] = passed[...]
    for p, read in enumerate(read_main):
        main[p, 0, BASE : BASE + N, :] = read(0, N)
        main[p, 0, BASE - 4 : BASE, :] = halo[0, 4 * p : 4 * p + 4, :]
        main[p, 0, BASE + N : BASE + N + 4, :] = halo[1, 4 * p : 4 * p + 4, :]
        turn[8 * p : 8 * p + 4, :] = sides[0, 4 * p : 4 * p + 4, :]
        turn[8 * p + 4 : 8 * p + 8, :] = sides[1, 4 * p : 4 * p + 4, :]
    for q, read in enumerate(read_extra):
        at, to = 4 * MAIN + 2 * q, 8 * MAIN + 4 * q
        extra[q, 0, BASE : BASE + N, :] = read(0, N)
        extra[q, 0, BASE - 2 : BASE, :] = halo[0, at : at + 2, :]
        extra[q, 0, BASE + N : BASE + N + 2, :] = halo[1, at : at + 2, :]
        turn[to : to + 2, :] = sides[0, at : at + 2, :]
        turn[to + 2 : to + 4, :] = sides[1, at : at + 2, :]
    at = 8 * MAIN + 4 * EXTRA
    turn[at:, :] = jnp.zeros((N - at, N), F32)
    turned = turn[...].T
    for p in range(MAIN):
        main[p, 1, BASE : BASE + N, :] = pltpu.roll(turned, (N - 4 - 8 * p) % N, 1)
    for q in range(EXTRA):
        extra[q, 1, BASE : BASE + N, :] = pltpu.roll(turned, (N - 2 - 8 * MAIN - 4 * q) % N, 1)
    turn[0:4, :] = sides[0, LINES : LINES + 4, :]
    turn[4:8, :] = sides[1, LINES : LINES + 4, :]
    turned = pltpu.roll(turn[...].T, N - 4, 1)
    for p in range(MAIN):
        main[p, 1, BASE - 4 : BASE, :] = turned[8 * p : 8 * p + 8][:4]
        main[p, 1, BASE + N : BASE + N + 4, :] = turned[8 * p : 8 * p + 8][4:]

    def shift(pair, s):
        a0, a1 = pair
        r0, r1 = pltpu.roll(a0, (-s) % N, 1), pltpu.roll(a1, (-s) % N, 1)
        inside = lane < N - s if s > 0 else lane >= -s
        return jnp.where(inside, r0, r1), jnp.where(inside, r1, r0)

    def load(ref, plane, row, dr=0):
        return tuple(ref[plane, i, pl.ds(row + dr, 8), :] for i in range(2))

    def save(ref, plane, row, pair):
        for i in range(2):
            ref[plane, i, pl.ds(row, 8), :] = pair[i]

    def each(function, *pairs):
        return tuple(function(*pair) for pair in zip(*pairs, strict=True))

    def face(blows, c2, c1, c0, cp):
        near_up = jnp.where(blows, c1, c0)
        far_up = jnp.where(blows, c2, cp)
        return 2.0 * (c0 + c1) + 3.0 * near_up - far_up

    def spread_east(blows, grads):
        plus = each(lambda p, x: jnp.where(p, x, 0.0), blows, grads)
        minus = each(lambda x, y: x - y, grads, plus)
        twice = each(lambda x: 2.0 * x, grads)
        after = each(lambda t, x, y: t + 3.0 * x - y, twice, plus, shift(plus, 1))
        before = each(lambda t, x, y: t + 3.0 * x - y, twice, minus, shift(minus, -1))
        return each(lambda x, y: x + y, shift(after, 1), before)

    def spread_north(winds, grads):
        total = 2.0 * (grads[1] + grads[2])
        total += 3.0 * (jnp.where(winds[2], grads[2], 0.0) + jnp.where(winds[1], 0.0, grads[1]))
        return total - jnp.where(winds[3], grads[3], 0.0) - jnp.where(winds[0], 0.0, grads[0])

    def prepare(t, carry):
        row = pl.multiple_of(t * 8, 8)
        rho = load(main, RHO, row)
        low = load(main, RHO, row, -1)
        left = shift(rho, -1)
        east, north = load(main, EAST, row), load(main, NORTH, row)
        save(mass, 0, row, each(lambda w, x, y: w * (x + y) * (1.0 / 12.0), east, rho, left))
        save(mass, 1, row, each(lambda w, x, y: w * (x + y) * (1.0 / 12.0), north, rho, low))
        scale = each(lambda x: COURANT / x, rho)
        save(inv, 0, row, scale)
        land = load(extra, BINS, row)
        for b in range(BINS):
            save(g, b, row, each(lambda x, y: x * y, load(main, BINS + b, row), scale))
            kept = each(lambda x: jnp.zeros_like(x), land)
            for kind in range(8):
                kept = each(lambda k, x: jnp.where(k == float(kind), deposition[kind, b], x), land, kept)
            save(keep, b, row, each(lambda x: 1.0 - TIME_STEP * x, kept))
        return carry

    lax.fori_loop(1, 19, prepare, 0)

    def first(t, carry):
        row = pl.multiple_of(t * 8, 8)
        blows_e = each(lambda w: w > 0.0, load(main, EAST, row))
        blows_n = each(lambda w: w > 0.0, load(main, NORTH, row))
        mass_e, mass_n, scale = load(mass, 0, row), load(mass, 1, row), load(inv, 0, row)
        for b in range(BINS):
            c = load(main, b, row)
            kept = load(keep, b, row)
            fe = each(lambda m, *x: m * face(*x), mass_e, blows_e, shift(c, -2), shift(c, -1), c, shift(c, 1))
            fn = each(
                lambda m, *x: m * face(*x),
                mass_n, blows_n, load(main, b, row, -2), load(main, b, row, -1), c, load(main, b, row, 1),
            )
            save(flux, b, row, fe)
            save(flux, BINS + b, row, fn)
            save(
                middle, b, row,
                each(lambda x, k, s, i, n, f: x * k + s - i * (n - f), c, kept, load(extra, b, row), scale, shift(fe, 1), fe),
            )
            gb = load(g, b, row)
            ge = each(lambda m, x, y: m * (x - y), mass_e, gb, shift(gb, -1))
            save(back, b, row, each(lambda m, x, y: m * (x - y), mass_n, gb, load(g, b, row, -1)))
            save(second, b, row, each(lambda f, k, s: f * k + s, load(main, BINS + b, row), kept, spread_east(blows_e, ge)))
        return carry

    lax.fori_loop(1, 19, first, 0)

    def join(t, carry):
        row = pl.multiple_of(t * 8, 8)
        winds = [each(lambda w: w > 0.0, load(main, NORTH, row, dr)) for dr in (-1, 0, 1, 2)]
        scale = load(inv, 0, row)
        for b in range(BINS):
            fn, up = load(flux, BINS + b, row), load(flux, BINS + b, row, 1)
            save(middle, b, row, each(lambda m, i, n, f: m - i * (n - f), load(middle, b, row), scale, up, fn))
            grads = [load(back, b, row, dr) for dr in (-1, 0, 1, 2)]
            whole = tuple(
                second[b, i, pl.ds(row, 8), :] + spread_north([w[i] for w in winds], [x[i] for x in grads]) for i in range(2)
            )
            save(second, b, row, whole)
            save(second, BINS + b, row, each(lambda m, i: m * i, whole, scale))
        return carry

    lax.fori_loop(1, 19, join, 0)

    def last(t, carry):
        row = pl.multiple_of(t * 8, 8)
        blows_e = each(lambda w: w > 0.0, load(main, EAST, row))
        blows_n = main[NORTH, 0, pl.ds(row, 8), :] > 0.0
        mass_e, mass_n = load(mass, 0, row), mass[1, 0, pl.ds(row, 8), :]
        rho = load(main, RHO, row)
        rim_e = rim_n = None
        own = 0.0
        for b in range(BINS):
            c = load(middle, b, row)
            fe = each(lambda m, *x: m * face(*x), mass_e, blows_e, shift(c, -2), shift(c, -1), c, shift(c, 1))
            rows = [middle[b, 0, pl.ds(row + dr, 8), :] for dr in (-2, -1, 1)]
            fn = mass_n * face(blows_n, rows[0], rows[1], c[0], rows[2])
            flux2[b, pl.ds(row, 8), :] = fn
            ga, gb = load(g, b, row), load(second, BINS + b, row)
            dea = each(lambda x, y: x - y, ga, shift(ga, -1))
            deb = each(lambda x, y: x - y, gb, shift(gb, -1))
            dna = ga[0] - g[b, 0, pl.ds(row - 1, 8), :]
            dnb = gb[0] - second[BINS + b, 0, pl.ds(row - 1, 8), :]
            old = load(flux, b, row)
            old_n = flux[BINS + b, 0, pl.ds(row, 8), :]
            add_e = each(lambda x, y, z, w: x * y + z * w, fe, dea, old, deb)
            add_n = fn * dna + old_n * dnb
            rim_e = add_e if rim_e is None else each(lambda x, y: x + y, rim_e, add_e)
            rim_n = add_n if rim_n is None else rim_n + add_n
            own = own + ga[0] * (shift(fe, 1)[0] - fe[0]) + gb[0] * (shift(old, 1)[0] - old[0])
            bank[b, pl.ds(row, 8), :] = mass_n * dnb
            ge = each(lambda m, x: m * x, mass_e, deb)
            moved = second[b, 0, pl.ds(row, 8), :] * keep[b, 0, pl.ds(row, 8), :]
            second[b, 0, pl.ds(row, 8), :] = moved + spread_east(blows_e, ge)[0]
        left = shift(rho, -1)
        rim_e = each(lambda x, a, b: x / (a + b), rim_e, rho, left)
        hn[pl.ds(row, 8), :] = rim_n / (rho[0] + main[RHO, 0, pl.ds(row - 1, 8), :])
        dens[0, pl.ds(row, 8), :] = own
        dens[1, pl.ds(row, 8), :] = rim_e[0] + shift(rim_e, 1)[0]
        return carry

    def emission(t, carry):
        row = pl.multiple_of(t * 8, 8)
        at = pl.multiple_of(t * 8 - BASE, 8)
        ground = (TIME_STEP * ins[8][pl.ds(at, 8), :].astype(F32))
        for b in range(BINS):
            total = main[BINS + b, 0, pl.ds(row, 8), :] + second[b, 0, pl.ds(row, 8), :]
            emis_out[b, pl.ds(at, 8), :] = ground * total
        return carry

    lax.fori_loop(2, 18, emission, 0)
    lax.fori_loop(1, 19, last, 0)

    def finish(t, carry):
        row = pl.multiple_of(t * 8, 8)
        at = pl.multiple_of(t * 8 - BASE, 8)
        winds = [main[NORTH, 0, pl.ds(row + dr, 8), :] > 0.0 for dr in (-1, 0, 1, 2)]
        own = dens[0, pl.ds(row, 8), :]
        for b in range(BINS):
            grads = [bank[b, pl.ds(row + dr, 8), :] for dr in (-1, 0, 1, 2)]
            adj_out[b, 0, pl.ds(at, 8), :] = second[b, 0, pl.ds(row, 8), :] + spread_north(winds, grads)
            ga, gb = g[b, 0, pl.ds(row, 8), :], second[BINS + b, 0, pl.ds(row, 8), :]
            own += ga * (flux2[b, pl.ds(row + 1, 8), :] - flux2[b, pl.ds(row, 8), :])
            own += gb * (flux[BINS + b, 0, pl.ds(row + 1, 8), :] - flux[BINS + b, 0, pl.ds(row, 8), :])
        total = own / main[RHO, 0, pl.ds(row, 8), :] + dens[1, pl.ds(row, 8), :]
        dens_out[0, pl.ds(at, 8), :] = total + hn[pl.ds(row, 8), :] + hn[pl.ds(row + 1, 8), :]
        return carry

    lax.fori_loop(2, 18, finish, 0)


def swaps(count, offset, closed):
    pairs = []
    for low in range(offset, count, 2):
        high = low + 1
        if high >= count and closed:
            continue
        pairs += [(low, high % count), (high % count, low)]
    return pairs


SMEM = pl.BlockSpec(memory_space=pltpu.SMEM)
VMEM = pl.BlockSpec(memory_space=pltpu.VMEM)


def kernel_call(body, smem_count, arrays, out_shapes, scratch, flops=0):
    return pl.pallas_call(
        body,
        out_shape=[jax.ShapeDtypeStruct(s, F32) for s in out_shapes],
        in_specs=[SMEM] * smem_count + [VMEM] * (len(arrays) - smem_count),
        out_specs=[VMEM] * len(out_shapes),
        scratch_shapes=[pltpu.VMEM(s, F32) for s in scratch],
        compiler_params=pltpu.CompilerParams(vmem_limit_bytes=40 * 1024 * 1024),
    )(*arrays)


def shards(*args):
    ins, deposition = args[:10], args[10]
    lat, lon = lax.axis_index("lat"), lax.axis_index("lon")
    lats, lons = lax.axis_size("lat"), lax.axis_size("lon")
    info = jnp.stack([lat % 2, lon % 2, (lat == 0).astype(jnp.int32), (lat == lats - 1).astype(jnp.int32)]).astype(jnp.int32)
    msg = (LAT_MSG, N)
    out0, out1, lines = kernel_call(
        pack_kernel, 1, (info, *ins), [msg, msg, (2, LON_MSG, N)], [(2, *msg), (N, N)]
    )
    got0 = lax.ppermute(out0, "lat", swaps(lats, 0, True))
    got1 = lax.ppermute(out1, "lat", swaps(lats, 1, True))
    (both,) = kernel_call(
        corner_kernel, 1, (info, got0, got1, lines), [(2 * LON_MSG, N)], [(2, *msg), (N, N)]
    )
    near = lax.ppermute(both, "lon", swaps(lons, 0, False))
    onward = [(i, (i + (2 if i % 2 == 0 else lons - 2)) % lons) for i in range(lons)]
    passed = lax.ppermute(near[LON_MSG:], "lon", onward)
    pair = (2, ROWS, N)
    outs = kernel_call(
        main_kernel,
        2,
        (info, deposition, *ins, got0, got1, near, passed),
        [(BINS, 1, N, N), (1, N, N), (BINS, N, N)],
        [
            (2, *msg),
            (2, LON_MSG, N),
            (N, N),
            (MAIN, *pair),
            (EXTRA, *pair),
            (2, *pair),
            (1, *pair),
            (BINS, *pair),
            (BINS, *pair),
            (BINS, *pair),
            (2 * BINS, *pair),
            (2 * BINS, *pair),
            (BINS, *pair),
            (BINS, ROWS, N),
            (BINS, ROWS, N),
            (ROWS, N),
            (2, ROWS, N),
        ],
    )
    return tuple(outs)


def solution(mesh):
    return jax.shard_map(
        shards,
        mesh=mesh,
        in_specs=(
            P(None, None, "lat", "lon"),
            P(None, None, "lat", "lon"),
            P(None, "lat", "lon"),
            P(None, "lat", "lon"),
            P(None, "lat", "lon"),
            P(None, "lat", "lon"),
            P(None, "lat", "lon"),
            P("lat", "lon"),
            P("lat", "lon"),
            P(None, "lat", "lon"),
            P(),
        ),
        out_specs=(P(None, None, "lat", "lon"), P(None, "lat", "lon"), P(None, "lat", "lon")),
        check_vma=False,
    )
```

```python
import jax
import jax.numpy as jnp
from jax import lax
from jax.experimental import pallas as pl
from jax.experimental.pallas import tpu as pltpu
from jax.sharding import PartitionSpec as P

COURANT = 0.3
TIME_STEP = 0.25

N = 128
BINS = 4
MAIN = 2 * BINS + 3
EXTRA = BINS + 1
EAST, NORTH, RHO = 2 * BINS, 2 * BINS + 1, 2 * BINS + 2
LINES = 4 * MAIN + 2 * EXTRA
LAT_MSG = 56
LON_MSG = 64
BASE = 16
ROWS = 160
OWN_FLOPS = 3_000_000
OWN_TALL, OWN_END = 24, 32
EDGE_TALL, EDGE_END = 48, 64
PLANES = MAIN + EXTRA + 1
GROUND = MAIN + EXTRA
F32 = jnp.float32


def position():
    lat, lon = lax.axis_index("lat"), lax.axis_index("lon")
    last = lax.axis_size("lat") - 1
    return lat % 2, lon % 2, (lat == 0).astype(jnp.int32), (lat == last).astype(jnp.int32)


def plane_readers(refs, info):
    tracer, adjoint, speed_e, speed_n, sign_e, sign_n, density, land, mask, emission = refs

    def east(at, size):
        s = speed_e[0, pl.ds(at, size), :]
        return jnp.where(sign_e[0, pl.ds(at, size), :] == 1, s, -s)

    def north(at, size):
        s = speed_n[0, pl.ds(at, size), :]
        s = jnp.where(sign_n[0, pl.ds(at, size), :] == 1, s, -s)
        row = lax.broadcasted_iota(jnp.int32, (size, N), 0) + at
        return jnp.where((row == 0) & (info[2] == 1), 0.0, s)

    def source(b):
        def read(at, size):
            m = mask[pl.ds(at, size), :].astype(F32)
            return TIME_STEP * m * emission[b, pl.ds(at, size), :]

        return read

    main = [lambda at, size, b=b: tracer[b, 0, pl.ds(at, size), :] for b in range(BINS)]
    main += [lambda at, size, b=b: adjoint[b, 0, pl.ds(at, size), :] for b in range(BINS)]
    main += [east, north, lambda at, size: density[0, pl.ds(at, size), :]]
    extra = [source(b) for b in range(BINS)]
    extra += [lambda at, size: land[pl.ds(at, size), :].astype(F32)]
    return main, extra


def pack_kernel(*refs):
    info = position()
    sources, (out0, out1, lines_out, planes), ins = refs[:10], refs[10:14], refs[14:24]
    edge, packed, sem = refs[24:]
    copies = [pltpu.make_async_copy(x, y, sem.at[i]) for i, (x, y) in enumerate(zip(sources, ins, strict=True))]
    for copy in copies:
        copy.start()
    for copy in copies:
        copy.wait()
    main, extra = plane_readers(ins, info)
    lane = lax.broadcasted_iota(jnp.int32, (N, N), 1)
    for p, read in enumerate(main + extra):
        planes[p] = read(0, N)
    planes[GROUND] = TIME_STEP * ins[8][...].astype(F32)
    for p in range(MAIN):
        edge[0, 4 * p : 4 * p + 4, :] = planes[p, 0:4, :]
        edge[1, 4 * p : 4 * p + 4, :] = planes[p, N - 4 :, :]
    for q in range(EXTRA):
        at = 4 * MAIN + 2 * q
        edge[0, at : at + 2, :] = planes[MAIN + q, 0:2, :]
        edge[1, at : at + 2, :] = planes[MAIN + q, N - 2 :, :]
    edge[:, LINES:LAT_MSG, :] = jnp.zeros((2, LAT_MSG - LINES, N), F32)
    parity = info[0]
    out0[...] = edge[1 - parity]
    out1[...] = edge[parity]
    both = jnp.zeros((N, N), F32)
    for p in range(MAIN):
        turned = pltpu.roll(planes[p], 8 * p + 4, 1)
        both = jnp.where((lane >= 8 * p) & (lane < 8 * p + 8), turned, both)
    for q in range(EXTRA):
        at = 8 * MAIN + 4 * q
        turned = pltpu.roll(planes[MAIN + q], at + 2, 1)
        both = jnp.where((lane >= at) & (lane < at + 4), turned, both)
    packed[...] = both.T
    for p in range(MAIN):
        lines_out[1, 4 * p : 4 * p + 4, :] = packed[8 * p : 8 * p + 4, :]
        lines_out[0, 4 * p : 4 * p + 4, :] = packed[8 * p + 4 : 8 * p + 8, :]
    for q in range(EXTRA):
        at, to = 8 * MAIN + 4 * q, 4 * MAIN + 2 * q
        lines_out[1, to : to + 2, :] = packed[at : at + 2, :]
        lines_out[0, to : to + 2, :] = packed[at + 2 : at + 4, :]
    lines_out[:, LINES:LON_MSG, :] = jnp.zeros((2, LON_MSG - LINES, N), F32)


def place_lat(info, got0, got1, halo):
    parity = info[0]
    halo[1 - parity] = got0[...]
    halo[parity] = got1[...]
    at = 4 * RHO

    @pl.when(info[2] == 1)
    def _():
        halo[0, at : at + 4, :] = jnp.ones((4, N), F32)

    @pl.when(info[3] == 1)
    def _():
        halo[1, at : at + 4, :] = jnp.ones((4, N), F32)


def corner_kernel(got0, got1, lines, out, halo, rows):
    info = position()
    place_lat(info, got0, got1, halo)
    rows[8 * MAIN :, :] = jnp.zeros((N - 8 * MAIN, N), F32)
    for p in range(MAIN):
        rows[8 * p : 8 * p + 4, :] = halo[0, 4 * p : 4 * p + 4, :]
        rows[8 * p + 4 : 8 * p + 8, :] = halo[1, 4 * p : 4 * p + 4, :]
    turned = rows[...].T
    parity = info[1]
    out[0:LON_MSG, :] = lines[1 - parity]
    out[LON_MSG:, :] = lines[parity]
    left, right = turned[0:8][:4], turned[N - 8 :][4:]

    @pl.when(parity == 0)
    def _():
        out[LINES : LINES + 4, :] = right
        out[LON_MSG + LINES : LON_MSG + LINES + 4, :] = left

    @pl.when(parity == 1)
    def _():
        out[LINES : LINES + 4, :] = left
        out[LON_MSG + LINES : LON_MSG + LINES + 4, :] = right


def shift(x, s):
    return pltpu.roll(x, (-s) % N, 1)


def face(blows, c2, c1, c0, cp):
    near_up = jnp.where(blows, c1, c0)
    far_up = jnp.where(blows, c2, cp)
    return 2.0 * (c0 + c1) + 3.0 * near_up - far_up


def spread_east(blows, grads):
    plus = jnp.where(blows, grads, 0.0)
    minus = grads - plus
    twice = 2.0 * grads
    after = twice + 3.0 * plus - shift(plus, 1)
    before = twice + 3.0 * minus - shift(minus, -1)
    return shift(after, 1) + before


def spread_north(winds, grads):
    total = 2.0 * (grads[1] + grads[2])
    total += 3.0 * (jnp.where(winds[2], grads[2], 0.0) + jnp.where(winds[1], 0.0, grads[1]))
    return total - jnp.where(winds[3], grads[3], 0.0) - jnp.where(winds[0], 0.0, grads[0])


def places(count):
    at, total = {}, 0
    for name, size in (("mass", 2), ("keep", count), ("g", count), ("middle", count), ("seen", count), ("gm", count), ("flux", 2 * count)):
        at[name] = total
        total += size
    return at, total


def first_half(tall, count, field_of, keep_of, state, back, scale_ref):
    field = field_of(tall)
    at, _ = places(count)

    def get(name, b, row):
        return state[at[name] + b, pl.ds(row, tall), :]

    def put(name, b, row, value):
        state[at[name] + b, pl.ds(row, tall), :] = value

    def prepare(t, carry):
        row = pl.multiple_of(8 + t * tall, 8)
        rho = field("rho", 0, row)
        put("mass", 0, row, field("east", 0, row) * (rho + shift(rho, -1)) * (1.0 / 12.0))
        put("mass", 1, row, field("north", 0, row) * (rho + field("rho", 0, row - 1)) * (1.0 / 12.0))
        scale = COURANT / rho
        scale_ref[pl.ds(row, tall), :] = scale
        for b, kept in enumerate(keep_of(row)):
            put("g", b, row, field("adjoint", b, row) * scale)
            put("keep", b, row, kept)
        return carry

    lax.fori_loop(0, 144 // tall, prepare, 0)

    def first(t, carry):
        row = pl.multiple_of(8 + t * tall, 8)
        blows_e, blows_n = field("east", 0, row) > 0.0, field("north", 0, row) > 0.0
        mass_e, mass_n, scale = get("mass", 0, row), get("mass", 1, row), scale_ref[pl.ds(row, tall), :]
        for b in range(count):
            c, kept = field("tracer", b, row), get("keep", b, row)
            fe = mass_e * face(blows_e, shift(c, -2), shift(c, -1), c, shift(c, 1))
            fn = mass_n * face(
                blows_n, field("tracer", b, row - 2), field("tracer", b, row - 1), c, field("tracer", b, row + 1)
            )
            put("flux", b, row, fe)
            put("flux", count + b, row, fn)
            put("middle", b, row, c * kept + field("source", b, row) - scale * (shift(fe, 1) - fe))
            gb = get("g", b, row)
            back[b, pl.ds(row, tall), :] = mass_n * (gb - get("g", b, row - 1))
            ge = mass_e * (gb - shift(gb, -1))
            put("seen", b, row, field("adjoint", b, row) * kept + spread_east(blows_e, ge))
        return carry

    lax.fori_loop(0, 144 // tall, first, 0)

    def join(t, carry):
        row = pl.multiple_of(8 + t * tall, 8)
        winds = [field("north", 0, row + dr) > 0.0 for dr in (-1, 0, 1, 2)]
        scale = scale_ref[pl.ds(row, tall), :]
        for b in range(count):
            change = get("flux", count + b, row + 1) - get("flux", count + b, row)
            put("middle", b, row, get("middle", b, row) - scale * change)
            whole = get("seen", b, row) + spread_north(winds, [back[b, pl.ds(row + dr, tall), :] for dr in (-1, 0, 1, 2)])
            put("seen", b, row, whole)
            put("gm", b, row, whole * scale)
        return carry

    lax.fori_loop(0, 144 // tall, join, 0)


def second_half(tall, end_tall, count, field_of, state, flux2, bank, part, rim, give):
    at, _ = places(count)
    field = field_of(tall)

    def get(name, b, row, size=tall):
        return state[at[name] + b, pl.ds(row, size), :]

    def last(t, carry):
        row = pl.multiple_of(8 + t * tall, 8)
        blows_e, blows_n = field("east", 0, row) > 0.0, field("north", 0, row) > 0.0
        mass_e, mass_n = get("mass", 0, row), get("mass", 1, row)
        rho = field("rho", 0, row)
        rim_e = rim_n = own = jnp.zeros((tall, N), F32)
        for b in range(count):
            c = get("middle", b, row)
            fe = mass_e * face(blows_e, shift(c, -2), shift(c, -1), c, shift(c, 1))
            fn = mass_n * face(blows_n, get("middle", b, row - 2), get("middle", b, row - 1), c, get("middle", b, row + 1))
            flux2[b, pl.ds(row, tall), :] = fn
            ga, gb = get("g", b, row), get("gm", b, row)
            old, old_n = get("flux", b, row), get("flux", count + b, row)
            deb = gb - shift(gb, -1)
            dnb = gb - get("gm", b, row - 1)
            rim_e += fe * (ga - shift(ga, -1)) + old * deb
            rim_n += fn * (ga - get("g", b, row - 1)) + old_n * dnb
            own += ga * (shift(fe, 1) - fe) + gb * (shift(old, 1) - old)
            bank[b, pl.ds(row, tall), :] = mass_n * dnb
            part[b, pl.ds(row, tall), :] = get("seen", b, row) * get("keep", b, row) + spread_east(blows_e, mass_e * deb)
        rim_e = rim_e / (rho + shift(rho, -1))
        rim[0, pl.ds(row, tall), :] = rim_n / (rho + field("rho", 0, row - 1))
        rim[1, pl.ds(row, tall), :] = own
        rim[2, pl.ds(row, tall), :] = rim_e + shift(rim_e, 1)
        return carry

    lax.fori_loop(0, 144 // tall, last, 0)

    def finish(t, carry):
        row = pl.multiple_of(BASE + t * end_tall, 8)
        field = field_of(end_tall)
        winds = [field("north", 0, row + dr) > 0.0 for dr in (-1, 0, 1, 2)]
        own = rim[1, pl.ds(row, end_tall), :]
        adjoints = []
        for b in range(count):
            grads = [bank[b, pl.ds(row + dr, end_tall), :] for dr in (-1, 0, 1, 2)]
            adjoints.append(part[b, pl.ds(row, end_tall), :] + spread_north(winds, grads))
            own += get("g", b, row, end_tall) * (flux2[b, pl.ds(row + 1, end_tall), :] - flux2[b, pl.ds(row, end_tall), :])
            own += get("gm", b, row, end_tall) * (get("flux", count + b, row + 1, end_tall) - get("flux", count + b, row, end_tall))
        total = own / field("rho", 0, row) + rim[2, pl.ds(row, end_tall), :] + rim[0, pl.ds(row, end_tall), :]
        seen = [field("adjoint", b, row) + get("seen", b, row, end_tall) for b in range(count)]
        give(row, pl.multiple_of(t * end_tall, 8), adjoints, total + rim[0, pl.ds(row + 1, end_tall), :], seen)
        return carry

    lax.fori_loop(0, N // end_tall, finish, 0)


PLACE = {"tracer": 0, "adjoint": BINS, "east": EAST, "north": NORTH, "rho": RHO, "source": MAIN, "land": MAIN + BINS}


def block_field(planes):
    return lambda tall: lambda name, b, row: planes[PLACE[name] + b, pl.ds(row, tall), :]


STRIPS = ("tracer", "adjoint", "source", "east", "north", "rho", "land")


def strip_field(strips):
    return lambda tall: lambda name, b, row: strips[STRIPS.index(name), pl.ds(row, tall), :]


def own_kernel(deposition, *refs):
    info = position()
    block, got0, got1, _, planes, state, strips, halo, back, scale = refs
    place_lat(info, got0, got1, halo)
    for p in range(MAIN):
        planes[p, BASE : BASE + N, :] = block[p]
        planes[p, BASE - 4 : BASE, :] = halo[0, 4 * p : 4 * p + 4, :]
        planes[p, BASE + N : BASE + N + 4, :] = halo[1, 4 * p : 4 * p + 4, :]
    for q in range(EXTRA):
        at, p = 4 * MAIN + 2 * q, MAIN + q
        planes[p, BASE : BASE + N, :] = block[p]
        planes[p, BASE - 2 : BASE, :] = halo[0, at : at + 2, :]
        planes[p, BASE + N : BASE + N + 2, :] = halo[1, at : at + 2, :]
    field = block_field(planes)(OWN_TALL)

    def keep_of(row):
        land = field("land", 0, row)
        for b in range(BINS):
            rate = jnp.zeros_like(land)
            for kind in range(8):
                rate = jnp.where(land == float(kind), deposition[b, kind], rate)
            yield 1.0 - TIME_STEP * rate

    first_half(OWN_TALL, BINS, block_field(planes), keep_of, state, back, scale)
    lane = lax.broadcasted_iota(jnp.int32, (OWN_TALL, N), 1)

    def cut(t, carry):
        row = pl.multiple_of(8 + t * OWN_TALL, 8)
        for i, name in enumerate(STRIPS):
            if name in ("tracer", "adjoint", "source"):
                both = jnp.zeros((OWN_TALL, N), F32)
                for b in range(BINS):
                    x, low = field(name, b, row), 32 * b
                    both = jnp.where((lane >= low) & (lane < low + 12), pltpu.roll(x, (low + 12) % N, 1), both)
                    both = jnp.where((lane >= low + 20) & (lane < low + 32), pltpu.roll(x, (low + 20) % N, 1), both)
            else:
                x = field(name, 0, row)
                both = jnp.where(lane < 12, pltpu.roll(x, 12, 1), 0.0)
                both = jnp.where((lane >= 20) & (lane < 32), pltpu.roll(x, 20, 1), both)
                both = jnp.where(lane % 64 < 32, both, pltpu.roll(both, 32, 1))
                both = jnp.where(lane < 64, both, pltpu.roll(both, 64, 1))
            strips[i, pl.ds(row, OWN_TALL), :] = both
        return carry

    lax.fori_loop(0, 144 // OWN_TALL, cut, 0)


def rest_kernel(planes, state, block, near, adj_out, dens_out, emis_out, flux2, bank, part, rim):
    del near

    def give(row, at, adjoints, dens, seen):
        ground = block[GROUND, pl.ds(at, OWN_END), :]
        for b in range(BINS):
            adj_out[b, 0, pl.ds(at, OWN_END), :] = adjoints[b]
            emis_out[b, pl.ds(at, OWN_END), :] = ground * seen[b]
        dens_out[0, pl.ds(at, OWN_END), :] = dens

    second_half(OWN_TALL, OWN_END, BINS, block_field(planes), state, flux2, bank, part, rim, give)


def edge_kernel(deposition, strips_in, near, passed, adj, dens, emis, block, *refs):
    adj_out, dens_out, emis_out, strips, sides, turn, state, back, scale, flux2, bank, part, rim = refs
    lane = lax.broadcasted_iota(jnp.int32, (8, N), 1)
    parity = position()[1]
    sides[1 - parity] = near[0:LON_MSG, :]
    sides[parity] = passed[...]
    tall = lax.broadcasted_iota(jnp.int32, (N, N), 1) % 32
    strips[:, 8:BASE, :] = strips_in[:, 8:BASE, :]
    strips[:, BASE + N : BASE + N + 8, :] = strips_in[:, BASE + N : BASE + N + 8, :]
    for i, name in enumerate(STRIPS):
        wide = 2 if name in ("source", "land") else 4
        inside = (tall >= 16 - wide - (4 - wide)) & (tall < 12 + wide) | (tall >= 20 - wide) & (tall < 20)
        for b in range(BINS):
            p = PLACE[name] + (b if name in ("tracer", "adjoint", "source") else 0)
            at = 4 * p if p < MAIN else 4 * MAIN + 2 * (p - MAIN)
            turn[i, 32 * b + 12 : 32 * b + 12 + wide, :] = sides[1, at : at + wide, :]
            turn[i, 32 * b + 20 - wide : 32 * b + 20, :] = sides[0, at : at + wide, :]
        strips[i, BASE : BASE + N, :] = jnp.where(inside, turn[i].T, strips_in[i, BASE : BASE + N, :])
    turn[0, 0:4, :] = sides[1, LINES : LINES + 4, :]
    turn[0, 4:8, :] = sides[0, LINES : LINES + 4, :]
    turned = turn[0].T
    for i, name in enumerate(STRIPS):
        if name in ("source", "land"):
            continue
        low, high = strips[i, BASE - 8 : BASE, :], strips[i, BASE + N : BASE + N + 8, :]
        sub = lax.broadcasted_iota(jnp.int32, (8, N), 0)
        for b in range(BINS):
            p = PLACE[name] + (b if name in ("tracer", "adjoint") else 0)
            eight = pltpu.roll(turned[8 * p : 8 * p + 8], 32 * b + 12, 1)
            inside = (lane >= 32 * b + 12) & (lane < 32 * b + 20)
            half = pltpu.roll(eight, 4, 0)
            low = jnp.where(inside & (sub >= 4), half, low)
            high = jnp.where(inside & (sub < 4), half, high)
        strips[i, BASE - 8 : BASE, :] = low
        strips[i, BASE + N : BASE + N + 8, :] = high
    field = strip_field(strips)(EDGE_TALL)
    lane = lax.broadcasted_iota(jnp.int32, (EDGE_TALL, N), 1)
    rates = []
    for kind in range(8):
        rate = jnp.where(lane < 32, deposition[0, kind], deposition[1, kind])
        rate = jnp.where(lane < 64, rate, jnp.where(lane < 96, deposition[2, kind], deposition[3, kind]))
        rates.append(rate)

    def keep_of(row):
        land = field("land", 0, row)
        rate = jnp.zeros_like(land)
        for kind in range(8):
            rate = jnp.where(land == float(kind), rates[kind], rate)
        yield 1.0 - TIME_STEP * rate

    first_half(EDGE_TALL, 1, strip_field(strips), keep_of, state, back, scale)
    lane = lax.broadcasted_iota(jnp.int32, (EDGE_END, N), 1)
    left, right = lane < 4, lane >= N - 4

    def patch(value, b, old):
        value_right = pltpu.roll(value, (116 - 32 * b) % N, 1)
        value_left = pltpu.roll(value, (-32 * b - 20) % N, 1)
        return jnp.where(left, value_left, jnp.where(right, value_right, old))

    def give(row, at, adjoints, total, seen):
        ground = block[GROUND, pl.ds(at, EDGE_END), :]
        for b in range(BINS):
            adj_out[b, 0, pl.ds(at, EDGE_END), :] = patch(adjoints[0], b, adj[b, 0, pl.ds(at, EDGE_END), :])
            old = emis[b, pl.ds(at, EDGE_END), :]
            emis_out[b, pl.ds(at, EDGE_END), :] = jnp.where(left | right, ground * patch(seen[0], b, old), old)
        total = total + pltpu.roll(total, 32, 1)
        total = total + pltpu.roll(total, 64, 1)
        dens_out[0, pl.ds(at, EDGE_END), :] = patch(total, 0, dens[0, pl.ds(at, EDGE_END), :])

    second_half(EDGE_TALL, EDGE_END, 1, strip_field(strips), state, flux2, bank, part, rim, give)


def swaps(count, offset, closed):
    pairs = []
    for low in range(offset, count, 2):
        high = low + 1
        if high >= count and closed:
            continue
        pairs += [(low, high % count), (high % count, low)]
    return pairs


SMEM = pl.BlockSpec(memory_space=pltpu.SMEM)
VMEM = pl.BlockSpec(memory_space=pltpu.VMEM)
HBM = pl.BlockSpec(memory_space=pltpu.HBM)


def kernel_call(body, smem, arrays, out_shapes, scratch, place=VMEM, extra=(), flops=0, fast=True):
    return pl.pallas_call(
        body,
        out_shape=[pltpu.VMEM(s, F32) if fast else jax.ShapeDtypeStruct(s, F32) for s in out_shapes],
        in_specs=[SMEM] * smem + [place] * (len(arrays) - smem),
        out_specs=[VMEM] * len(out_shapes),
        scratch_shapes=[pltpu.VMEM(s, F32) for s in scratch] + list(extra),
        compiler_params=pltpu.CompilerParams(vmem_limit_bytes=24 * 1024 * 1024),
        cost_estimate=pl.CostEstimate(flops=flops, bytes_accessed=0, transcendentals=0) if flops else None,
    )(*arrays)


def shards(*args):
    ins, deposition = args[:10], args[10].T
    lats, lons = lax.axis_size("lat"), lax.axis_size("lon")
    msg = (LAT_MSG, N)
    ins = [pltpu.with_memory_space_constraint(x, pltpu.HBM) for x in ins]
    out0, out1, lines, block = kernel_call(
        pack_kernel,
        0,
        ins,
        [msg, msg, (2, LON_MSG, N), (PLANES, N, N)],
        [],
        HBM,
        [pltpu.VMEM(x.shape, x.dtype) for x in ins]
        + [pltpu.VMEM((2, *msg), F32), pltpu.VMEM((N, N), F32), pltpu.SemaphoreType.DMA((10,))],
    )
    got0 = lax.ppermute(out0, "lat", swaps(lats, 0, True))
    got1 = lax.ppermute(out1, "lat", swaps(lats, 1, True))
    (both,) = kernel_call(corner_kernel, 0, (got0, got1, lines), [(2 * LON_MSG, N)], [(2, *msg), (N, N)])
    near = lax.ppermute(both, "lon", swaps(lons, 0, False))
    plane = (ROWS, N)
    planes, state, strips = kernel_call(
        own_kernel,
        1,
        (deposition, block, got0, got1, both),
        [(MAIN + EXTRA, *plane), (places(BINS)[1], *plane), (len(STRIPS), *plane)],
        [(2, *msg), (BINS, *plane), plane],
        flops=OWN_FLOPS,
    )
    onward = [(i, (i + (2 if i % 2 == 0 else lons - 2)) % lons) for i in range(lons)]
    near, strips = lax.optimization_barrier((near, strips))
    passed = lax.ppermute(near[LON_MSG:], "lon", onward)
    shapes = [(BINS, 1, N, N), (1, N, N), (BINS, N, N)]
    adj, dens, emis = kernel_call(
        rest_kernel,
        0,
        (planes, state, block, near),
        shapes,
        [(BINS, *plane), (BINS, *plane), (BINS, *plane), (3, *plane)],
        flops=OWN_FLOPS,
    )
    outs = kernel_call(
        edge_kernel,
        1,
        (deposition, strips, near, passed, adj, dens, emis, block),
        shapes,
        [
            (len(STRIPS), *plane),
            (2, LON_MSG, N),
            (len(STRIPS), N, N),
            (places(1)[1], *plane),
            (1, *plane),
            plane,
            (1, *plane),
            (1, *plane),
            (1, *plane),
            (3, *plane),
        ],
        fast=False,
    )
    return tuple(outs)


def solution(mesh):
    return jax.shard_map(
        shards,
        mesh=mesh,
        in_specs=(
            P(None, None, "lat", "lon"),
            P(None, None, "lat", "lon"),
            P(None, "lat", "lon"),
            P(None, "lat", "lon"),
            P(None, "lat", "lon"),
            P(None, "lat", "lon"),
            P(None, "lat", "lon"),
            P("lat", "lon"),
            P("lat", "lon"),
            P(None, "lat", "lon"),
            P(),
        ),
        out_specs=(P(None, None, "lat", "lon"), P(None, "lat", "lon"), P(None, "lat", "lon")),
        check_vma=False,
    )
```

```python
import jax
import jax.numpy as jnp
from jax import lax
from jax.experimental import pallas as pl
from jax.experimental.pallas import tpu as pltpu
from jax.sharding import PartitionSpec as P

COURANT = 0.3
TIME_STEP = 0.25

N = 128
BINS = 4
MAIN = 2 * BINS + 3
EXTRA = BINS + 1
EAST, NORTH, RHO = 2 * BINS, 2 * BINS + 1, 2 * BINS + 2
LINES = 4 * MAIN + 2 * EXTRA
LAT_MSG = 56
LON_MSG = 56
BASE = 16
ROWS = 160
OWN_FLOPS = 3_000_000
OWN_TALL, FIRST_TALL = 48, 48
REST_TALL, REST_END = 24, 32
EARLY = 10
EDGE_TALL, EDGE_END = 144, 128
PLANES = MAIN + EXTRA + 1
GROUND = MAIN + EXTRA
F32 = jnp.float32


def position():
    lat, lon = lax.axis_index("lat"), lax.axis_index("lon")
    last = lax.axis_size("lat") - 1
    return lat % 2, lon % 2, (lat == 0).astype(jnp.int32), (lat == last).astype(jnp.int32)


def plane_readers(refs, info):
    tracer, adjoint, speed_e, speed_n, sign_e, sign_n, density, land, mask, emission = refs

    def east(at, size):
        s = speed_e[0, pl.ds(at, size), :]
        return jnp.where(sign_e[0, pl.ds(at, size), :] == 1, s, -s)

    def north(at, size):
        s = speed_n[0, pl.ds(at, size), :]
        s = jnp.where(sign_n[0, pl.ds(at, size), :] == 1, s, -s)
        row = lax.broadcasted_iota(jnp.int32, (size, N), 0) + at
        return jnp.where((row == 0) & (info[2] == 1), 0.0, s)

    def source(b):
        def read(at, size):
            m = mask[pl.ds(at, size), :].astype(F32)
            return TIME_STEP * m * emission[b, pl.ds(at, size), :]

        return read

    main = [lambda at, size, b=b: tracer[b, 0, pl.ds(at, size), :] for b in range(BINS)]
    main += [lambda at, size, b=b: adjoint[b, 0, pl.ds(at, size), :] for b in range(BINS)]
    main += [east, north, lambda at, size: density[0, pl.ds(at, size), :]]
    extra = [source(b) for b in range(BINS)]
    extra += [lambda at, size: land[pl.ds(at, size), :].astype(F32)]
    return main, extra


def pack_kernel(*refs):
    info = position()
    sources, (out0, out1, lines_out, planes), ins = refs[:10], refs[10:14], refs[14:24]
    edge, packed, sem = refs[24:]
    copies = [pltpu.make_async_copy(x, y, sem.at[i]) for i, (x, y) in enumerate(zip(sources, ins, strict=True))]
    for copy in copies:
        copy.start()
    for copy in copies:
        copy.wait()
    main, extra = plane_readers(ins, info)
    lane = lax.broadcasted_iota(jnp.int32, (N, N), 1)
    for p, read in enumerate(main + extra):
        planes[p] = read(0, N)
    planes[GROUND] = TIME_STEP * ins[8][...].astype(F32)
    for p in range(MAIN):
        edge[0, 4 * p : 4 * p + 4, :] = planes[p, 0:4, :]
        edge[1, 4 * p : 4 * p + 4, :] = planes[p, N - 4 :, :]
    for q in range(EXTRA):
        at = 4 * MAIN + 2 * q
        edge[0, at : at + 2, :] = planes[MAIN + q, 0:2, :]
        edge[1, at : at + 2, :] = planes[MAIN + q, N - 2 :, :]
    edge[:, LINES:LAT_MSG, :] = jnp.zeros((2, LAT_MSG - LINES, N), F32)
    parity = info[0]
    out0[...] = edge[1 - parity]
    out1[...] = edge[parity]
    both = jnp.zeros((N, N), F32)
    for p in range(MAIN):
        turned = pltpu.roll(planes[p], 8 * p + 4, 1)
        both = jnp.where((lane >= 8 * p) & (lane < 8 * p + 8), turned, both)
    for q in range(EXTRA):
        at = 8 * MAIN + 4 * q
        turned = pltpu.roll(planes[MAIN + q], at + 2, 1)
        both = jnp.where((lane >= at) & (lane < at + 4), turned, both)
    packed[...] = both.T
    for p in range(MAIN):
        lines_out[1, 4 * p : 4 * p + 4, :] = packed[8 * p : 8 * p + 4, :]
        lines_out[0, 4 * p : 4 * p + 4, :] = packed[8 * p + 4 : 8 * p + 8, :]
    for q in range(EXTRA):
        at, to = 8 * MAIN + 4 * q, 4 * MAIN + 2 * q
        lines_out[1, to : to + 2, :] = packed[at : at + 2, :]
        lines_out[0, to : to + 2, :] = packed[at + 2 : at + 4, :]
    lines_out[:, LINES:LON_MSG, :] = jnp.zeros((2, LON_MSG - LINES, N), F32)


def place_lat(info, got0, got1, halo):
    parity = info[0]
    halo[1 - parity] = got0[1 - parity]
    halo[parity] = got1[...]
    at = 4 * RHO

    @pl.when(info[2] == 1)
    def _():
        halo[0, at : at + 4, :] = jnp.ones((4, N), F32)

    @pl.when(info[3] == 1)
    def _():
        halo[1, at : at + 4, :] = jnp.ones((4, N), F32)


def corner_kernel(got1, got0, lines, out, halo, rows):
    info = position()
    place_lat(info, got0, got1, halo)
    rows[8 * MAIN :, :] = jnp.zeros((N - 8 * MAIN, N), F32)
    for p in range(MAIN):
        rows[8 * p : 8 * p + 4, :] = halo[0, 4 * p : 4 * p + 4, :]
        rows[8 * p + 4 : 8 * p + 8, :] = halo[1, 4 * p : 4 * p + 4, :]
    turned = rows[...].T
    parity = info[1]
    out[0:LON_MSG, :] = lines[1 - parity]
    out[LON_MSG:, :] = lines[parity]
    left, right = turned[0:8][:2], turned[N - 8 :][6:]

    @pl.when(parity == 0)
    def _():
        out[LINES : LON_MSG, :] = right
        out[LON_MSG + LINES : 2 * LON_MSG, :] = left

    @pl.when(parity == 1)
    def _():
        out[LINES : LON_MSG, :] = left
        out[LON_MSG + LINES : 2 * LON_MSG, :] = right


def shift(x, s):
    return pltpu.roll(x, (-s) % N, 1)


def face(blows, c2, c1, c0, cp):
    near_up = jnp.where(blows, c1, c0)
    far_up = jnp.where(blows, c2, cp)
    return 2.0 * (c0 + c1) + 3.0 * near_up - far_up


def spread_east(blows, grads):
    plus = jnp.where(blows, grads, 0.0)
    minus = grads - plus
    twice = 2.0 * grads
    after = twice + 3.0 * plus - shift(plus, 1)
    before = twice + 3.0 * minus - shift(minus, -1)
    return shift(after, 1) + before


def spread_north(winds, grads):
    total = 2.0 * (grads[1] + grads[2])
    total += 3.0 * (jnp.where(winds[2], grads[2], 0.0) + jnp.where(winds[1], 0.0, grads[1]))
    return total - jnp.where(winds[3], grads[3], 0.0) - jnp.where(winds[0], 0.0, grads[0])


def lay(sizes):
    at, total = {}, 0
    for name, size in sizes:
        at[name] = total
        total += size
    return at, total


def places(count):
    return lay((("mass", 2), ("scale", 1), ("keep", count), ("g", count)))


def results(count):
    return lay((("middle", count), ("seen", count), ("gm", count), ("flux", 2 * count)))


def prepare_half(tall, count, field_of, keep_of, state):
    field = field_of(tall)
    at, _ = places(count)

    def put(name, b, row, value):
        state[at[name] + b, pl.ds(row, tall), :] = value

    def prepare(t, carry):
        row = pl.multiple_of(8 + t * tall, 8)
        rho = field("rho", 0, row)
        put("mass", 0, row, field("east", 0, row) * (rho + shift(rho, -1)) * (1.0 / 12.0))
        put("mass", 1, row, field("north", 0, row) * (rho + field("rho", 0, row - 1)) * (1.0 / 12.0))
        scale = COURANT / rho
        put("scale", 0, row, scale)
        for b, kept in enumerate(keep_of(row)):
            put("g", b, row, field("adjoint", b, row) * scale)
            put("keep", b, row, kept)
        return carry

    lax.fori_loop(0, 144 // tall, prepare, 0)


def first_half(tall, count, field_of, start, state, back):
    field = field_of(tall)
    at, _ = places(count)
    to, _ = results(count)

    def get(name, b, row):
        if name in at:
            return start[at[name] + b, pl.ds(row, tall), :]
        return state[to[name] + b, pl.ds(row, tall), :]

    def put(name, b, row, value):
        state[to[name] + b, pl.ds(row, tall), :] = value

    def first(t, carry):
        row = pl.multiple_of(8 + t * tall, 8)
        blows_e, blows_n = field("east", 0, row) > 0.0, field("north", 0, row) > 0.0
        mass_e, mass_n, scale = get("mass", 0, row), get("mass", 1, row), get("scale", 0, row)
        for b in range(count):
            c, kept = field("tracer", b, row), get("keep", b, row)
            fe = mass_e * face(blows_e, shift(c, -2), shift(c, -1), c, shift(c, 1))
            fn = mass_n * face(
                blows_n, field("tracer", b, row - 2), field("tracer", b, row - 1), c, field("tracer", b, row + 1)
            )
            put("flux", b, row, fe)
            put("flux", count + b, row, fn)
            put("middle", b, row, c * kept + field("source", b, row) - scale * (shift(fe, 1) - fe))
            gb = get("g", b, row)
            back[b, pl.ds(row, tall), :] = mass_n * (gb - get("g", b, row - 1))
            ge = mass_e * (gb - shift(gb, -1))
            put("seen", b, row, field("adjoint", b, row) * kept + spread_east(blows_e, ge))
        return carry

    lax.fori_loop(0, 144 // tall, first, 0)

    def join(t, carry):
        row = pl.multiple_of(8 + t * tall, 8)
        winds = [field("north", 0, row + dr) > 0.0 for dr in (-1, 0, 1, 2)]
        scale = get("scale", 0, row)
        for b in range(count):
            change = get("flux", count + b, row + 1) - get("flux", count + b, row)
            put("middle", b, row, get("middle", b, row) - scale * change)
            whole = get("seen", b, row) + spread_north(winds, [back[b, pl.ds(row + dr, tall), :] for dr in (-1, 0, 1, 2)])
            put("seen", b, row, whole)
            put("gm", b, row, whole * scale)
        return carry

    lax.fori_loop(0, 144 // tall, join, 0)


def second_half(tall, end_tall, count, field_of, start, state, flux2, bank, part, rim, give):
    at, _ = places(count)
    to, _ = results(count)
    field = field_of(tall)

    def get(name, b, row, size=tall):
        if name in at:
            return start[at[name] + b, pl.ds(row, size), :]
        return state[to[name] + b, pl.ds(row, size), :]

    def last(t, carry):
        row = pl.multiple_of(8 + t * tall, 8)
        blows_e, blows_n = field("east", 0, row) > 0.0, field("north", 0, row) > 0.0
        mass_e, mass_n = get("mass", 0, row), get("mass", 1, row)
        rho = field("rho", 0, row)
        rim_e = rim_n = own = jnp.zeros((tall, N), F32)
        for b in range(count):
            c = get("middle", b, row)
            fe = mass_e * face(blows_e, shift(c, -2), shift(c, -1), c, shift(c, 1))
            fn = mass_n * face(blows_n, get("middle", b, row - 2), get("middle", b, row - 1), c, get("middle", b, row + 1))
            flux2[b, pl.ds(row, tall), :] = fn
            ga, gb = get("g", b, row), get("gm", b, row)
            old, old_n = get("flux", b, row), get("flux", count + b, row)
            deb = gb - shift(gb, -1)
            dnb = gb - get("gm", b, row - 1)
            rim_e += fe * (ga - shift(ga, -1)) + old * deb
            rim_n += fn * (ga - get("g", b, row - 1)) + old_n * dnb
            own += ga * (shift(fe, 1) - fe) + gb * (shift(old, 1) - old)
            bank[b, pl.ds(row, tall), :] = mass_n * dnb
            part[b, pl.ds(row, tall), :] = get("seen", b, row) * get("keep", b, row) + spread_east(blows_e, mass_e * deb)
        rim_e = rim_e / (rho + shift(rho, -1))
        rim[0, pl.ds(row, tall), :] = rim_n / (rho + field("rho", 0, row - 1))
        rim[1, pl.ds(row, tall), :] = own
        rim[2, pl.ds(row, tall), :] = rim_e + shift(rim_e, 1)
        return carry

    lax.fori_loop(0, 144 // tall, last, 0)

    def finish(t, carry):
        row = pl.multiple_of(BASE + t * end_tall, 8)
        field = field_of(end_tall)
        winds = [field("north", 0, row + dr) > 0.0 for dr in (-1, 0, 1, 2)]
        own = rim[1, pl.ds(row, end_tall), :]
        adjoints = []
        for b in range(count):
            grads = [bank[b, pl.ds(row + dr, end_tall), :] for dr in (-1, 0, 1, 2)]
            adjoints.append(part[b, pl.ds(row, end_tall), :] + spread_north(winds, grads))
            own += get("g", b, row, end_tall) * (flux2[b, pl.ds(row + 1, end_tall), :] - flux2[b, pl.ds(row, end_tall), :])
            own += get("gm", b, row, end_tall) * (get("flux", count + b, row + 1, end_tall) - get("flux", count + b, row, end_tall))
        total = own / field("rho", 0, row) + rim[2, pl.ds(row, end_tall), :] + rim[0, pl.ds(row, end_tall), :]
        seen = [field("adjoint", b, row) + get("seen", b, row, end_tall) for b in range(count)]
        give(row, pl.multiple_of(t * end_tall, 8), adjoints, total + rim[0, pl.ds(row + 1, end_tall), :], seen)
        return carry

    lax.fori_loop(0, N // end_tall, finish, 0)


PLACE = {"tracer": 0, "adjoint": BINS, "east": EAST, "north": NORTH, "rho": RHO, "source": MAIN, "land": MAIN + BINS}


def block_field(planes):
    return lambda tall: lambda name, b, row: planes[PLACE[name] + b, pl.ds(row, tall), :]


STRIPS = ("tracer", "adjoint", "source", "east", "north", "rho", "land")


def strip_field(strips):
    return lambda tall: lambda name, b, row: strips[STRIPS.index(name), pl.ds(row, tall), :]


def own_kernel(deposition, *refs):
    info = position()
    block, got0, got1, _, planes, start, strips, *outs, halo = refs[:11]
    work = refs[11:]
    place_lat(info, got0, got1, halo)
    for p in range(MAIN):
        planes[p, BASE : BASE + N, :] = block[p]
        planes[p, BASE - 4 : BASE, :] = halo[0, 4 * p : 4 * p + 4, :]
        planes[p, BASE + N : BASE + N + 4, :] = halo[1, 4 * p : 4 * p + 4, :]
    for q in range(EXTRA):
        at, p = 4 * MAIN + 2 * q, MAIN + q
        planes[p, BASE : BASE + N, :] = block[p]
        planes[p, BASE - 2 : BASE, :] = halo[0, at : at + 2, :]
        planes[p, BASE + N : BASE + N + 2, :] = halo[1, at : at + 2, :]
    field = block_field(planes)(OWN_TALL)

    def keep_of(row):
        land = field("land", 0, row)
        for b in range(BINS):
            rate = jnp.zeros_like(land)
            for kind in range(8):
                rate = jnp.where(land == float(kind), deposition[b, kind], rate)
            yield 1.0 - TIME_STEP * rate

    prepare_half(OWN_TALL, BINS, block_field(planes), keep_of, start)
    lane = lax.broadcasted_iota(jnp.int32, (OWN_TALL, N), 1)

    def cut(t, carry):
        row = pl.multiple_of(8 + t * OWN_TALL, 8)
        for i, name in enumerate(STRIPS):
            if name in ("tracer", "adjoint", "source"):
                both = jnp.zeros((OWN_TALL, N), F32)
                for b in range(BINS):
                    x, low = field(name, b, row), 32 * b
                    both = jnp.where((lane >= low) & (lane < low + 12), pltpu.roll(x, (low + 12) % N, 1), both)
                    both = jnp.where((lane >= low + 20) & (lane < low + 32), pltpu.roll(x, (low + 20) % N, 1), both)
            else:
                x = field(name, 0, row)
                both = jnp.where(lane < 12, pltpu.roll(x, 12, 1), 0.0)
                both = jnp.where((lane >= 20) & (lane < 32), pltpu.roll(x, 20, 1), both)
                both = jnp.where(lane % 64 < 32, both, pltpu.roll(both, 32, 1))
                both = jnp.where(lane < 64, both, pltpu.roll(both, 64, 1))
            strips[i, pl.ds(row, OWN_TALL), :] = both
        return carry

    lax.fori_loop(0, 144 // OWN_TALL, cut, 0)

    @pl.when(runs_early())
    def _():
        both_halves(planes, start, block, outs, work)


def runs_early():
    return (lax.axis_index("lon") % 2 == 1) | (lax.axis_index("lat") >= EARLY * lax.axis_size("lat") // 16)


def both_halves(planes, start, block, outs, work):
    adj_out, dens_out, emis_out = outs
    state, back, flux2, bank, part, rim = work
    first_half(FIRST_TALL, BINS, block_field(planes), start, state, back)

    def give(row, at, adjoints, dens, seen):
        ground = block[GROUND, pl.ds(at, REST_END), :]
        for b in range(BINS):
            adj_out[b, 0, pl.ds(at, REST_END), :] = adjoints[b]
            emis_out[b, pl.ds(at, REST_END), :] = ground * seen[b]
        dens_out[0, pl.ds(at, REST_END), :] = dens

    second_half(REST_TALL, REST_END, BINS, block_field(planes), start, state, flux2, bank, part, rim, give)


def rest_kernel(planes, start, block, near, *refs):
    del near

    @pl.when(jnp.logical_not(runs_early()))
    def _():
        both_halves(planes, start, block, refs[3:6], refs[6:])


def edge_kernel(deposition, strips_in, near, passed, adj, dens, emis, block, *refs):
    adj_out, dens_out, emis_out, strips, sides, turn, start, state, back, flux2, bank, part, rim = refs
    lane = lax.broadcasted_iota(jnp.int32, (8, N), 1)
    parity = position()[1]
    sides[1 - parity] = near[0:LON_MSG, :]
    sides[parity] = passed[...]
    tall = lax.broadcasted_iota(jnp.int32, (N, N), 1) % 32
    strips[:, 8:BASE, :] = strips_in[:, 8:BASE, :]
    strips[:, BASE + N : BASE + N + 8, :] = strips_in[:, BASE + N : BASE + N + 8, :]
    for i, name in enumerate(STRIPS):
        wide = 2 if name in ("source", "land") else 4
        inside = (tall >= 16 - wide - (4 - wide)) & (tall < 12 + wide) | (tall >= 20 - wide) & (tall < 20)
        for b in range(BINS):
            p = PLACE[name] + (b if name in ("tracer", "adjoint", "source") else 0)
            at = 4 * p if p < MAIN else 4 * MAIN + 2 * (p - MAIN)
            turn[i, 32 * b + 12 : 32 * b + 12 + wide, :] = sides[1, at : at + wide, :]
            turn[i, 32 * b + 20 - wide : 32 * b + 20, :] = sides[0, at : at + wide, :]
        strips[i, BASE : BASE + N, :] = jnp.where(inside, turn[i].T, strips_in[i, BASE : BASE + N, :])
    turn[0, 0:2, :] = sides[1, LINES:LON_MSG, :]
    turn[0, 6:8, :] = sides[0, LINES:LON_MSG, :]
    turned = turn[0].T
    for i, name in enumerate(STRIPS):
        if name in ("source", "land"):
            continue
        low, high = strips[i, BASE - 8 : BASE, :], strips[i, BASE + N : BASE + N + 8, :]
        sub = lax.broadcasted_iota(jnp.int32, (8, N), 0)
        for b in range(BINS):
            p = PLACE[name] + (b if name in ("tracer", "adjoint") else 0)
            eight = pltpu.roll(turned[8 * p : 8 * p + 8], 32 * b + 12, 1)
            inside = (lane >= 32 * b + 12) & (lane < 32 * b + 20)
            half = pltpu.roll(eight, 4, 0)
            low = jnp.where(inside & (sub >= 4), half, low)
            high = jnp.where(inside & (sub < 4), half, high)
        strips[i, BASE - 8 : BASE, :] = low
        strips[i, BASE + N : BASE + N + 8, :] = high
    field = strip_field(strips)(EDGE_TALL)
    lane = lax.broadcasted_iota(jnp.int32, (EDGE_TALL, N), 1)
    rates = []
    for kind in range(8):
        rate = jnp.where(lane < 32, deposition[0, kind], deposition[1, kind])
        rate = jnp.where(lane < 64, rate, jnp.where(lane < 96, deposition[2, kind], deposition[3, kind]))
        rates.append(rate)

    def keep_of(row):
        land = field("land", 0, row)
        rate = jnp.zeros_like(land)
        for kind in range(8):
            rate = jnp.where(land == float(kind), rates[kind], rate)
        yield 1.0 - TIME_STEP * rate

    prepare_half(EDGE_TALL, 1, strip_field(strips), keep_of, start)
    first_half(EDGE_TALL, 1, strip_field(strips), start, state, back)
    lane = lax.broadcasted_iota(jnp.int32, (EDGE_END, N), 1)
    left, right = lane < 4, lane >= N - 4

    def patch(value, b, old):
        value_right = pltpu.roll(value, (116 - 32 * b) % N, 1)
        value_left = pltpu.roll(value, (-32 * b - 20) % N, 1)
        return jnp.where(left, value_left, jnp.where(right, value_right, old))

    def give(row, at, adjoints, total, seen):
        ground = block[GROUND, pl.ds(at, EDGE_END), :]
        for b in range(BINS):
            adj_out[b, 0, pl.ds(at, EDGE_END), :] = patch(adjoints[0], b, adj[b, 0, pl.ds(at, EDGE_END), :])
            old = emis[b, pl.ds(at, EDGE_END), :]
            emis_out[b, pl.ds(at, EDGE_END), :] = jnp.where(left | right, ground * patch(seen[0], b, old), old)
        total = total + pltpu.roll(total, 32, 1)
        total = total + pltpu.roll(total, 64, 1)
        dens_out[0, pl.ds(at, EDGE_END), :] = patch(total, 0, dens[0, pl.ds(at, EDGE_END), :])

    second_half(EDGE_TALL, EDGE_END, 1, strip_field(strips), start, state, flux2, bank, part, rim, give)


def swaps(count, offset, closed):
    pairs = []
    for low in range(offset, count, 2):
        high = low + 1
        if high >= count and closed:
            continue
        pairs += [(low, high % count), (high % count, low)]
    return pairs


SMEM = pl.BlockSpec(memory_space=pltpu.SMEM)
VMEM = pl.BlockSpec(memory_space=pltpu.VMEM)
HBM = pl.BlockSpec(memory_space=pltpu.HBM)


def kernel_call(body, smem, arrays, out_shapes, scratch, place=VMEM, extra=(), flops=0, fast=True, aliases=None):
    return pl.pallas_call(
        body,
        out_shape=[pltpu.VMEM(s, F32) if fast else jax.ShapeDtypeStruct(s, F32) for s in out_shapes],
        in_specs=[SMEM] * smem + [place] * (len(arrays) - smem),
        out_specs=[VMEM] * len(out_shapes),
        scratch_shapes=[pltpu.VMEM(s, F32) for s in scratch] + list(extra),
        input_output_aliases=aliases or {},
        compiler_params=pltpu.CompilerParams(vmem_limit_bytes=24 * 1024 * 1024),
        cost_estimate=pl.CostEstimate(flops=flops, bytes_accessed=0, transcendentals=0) if flops else None,
    )(*arrays)


def shards(*args):
    ins, deposition = args[:10], args[10].T
    lats, lons = lax.axis_size("lat"), lax.axis_size("lon")
    msg = (LAT_MSG, N)
    ins = [pltpu.with_memory_space_constraint(x, pltpu.HBM) for x in ins]
    out0, out1, lines, block = kernel_call(
        pack_kernel,
        0,
        ins,
        [msg, msg, (2, LON_MSG, N), (PLANES, N, N)],
        [],
        HBM,
        [pltpu.VMEM(x.shape, x.dtype) for x in ins]
        + [pltpu.VMEM((2, *msg), F32), pltpu.VMEM((N, N), F32), pltpu.SemaphoreType.DMA((10,))],
    )
    got1 = lax.ppermute(out1, "lat", swaps(lats, 1, True))
    got0 = lax.all_gather(out0, "lat", axis_index_groups=[[i, i + 1] for i in range(0, lats, 2)])
    (both,) = kernel_call(corner_kernel, 0, (got1, got0, lines), [(2 * LON_MSG, N)], [(2, *msg), (N, N)])
    near = lax.ppermute(both, "lon", swaps(lons, 0, False))
    plane = (ROWS, N)
    shapes = [(BINS, 1, N, N), (1, N, N), (BINS, N, N)]
    work = [(results(BINS)[1], *plane)] + [(BINS, *plane)] * 4 + [(3, *plane)]
    planes, start, strips, *first_outs = kernel_call(
        own_kernel,
        1,
        (deposition, block, got0, got1, both),
        [(MAIN + EXTRA, *plane), (places(BINS)[1], *plane), (len(STRIPS), *plane), *shapes],
        [(2, *msg), *work],
        flops=OWN_FLOPS,
    )
    onward = [(i, (i + (2 if i % 2 == 0 else lons - 2)) % lons) for i in range(lons)]
    near, strips = lax.optimization_barrier((near, strips))
    passed = lax.ppermute(near[LON_MSG:], "lon", onward)
    adj, dens, emis = kernel_call(
        rest_kernel,
        0,
        (planes, start, block, near, *first_outs),
        shapes,
        work,
        aliases={4: 0, 5: 1, 6: 2},
        flops=OWN_FLOPS,
    )
    outs = kernel_call(
        edge_kernel,
        1,
        (deposition, strips, near, passed, adj, dens, emis, block),
        shapes,
        [
            (len(STRIPS), *plane),
            (2, LON_MSG, N),
            (len(STRIPS), N, N),
            (places(1)[1], *plane),
            (results(1)[1], *plane),
            (1, *plane),
            (1, *plane),
            (1, *plane),
            (1, *plane),
            (3, *plane),
        ],
        fast=False,
    )
    return tuple(outs)


def solution(mesh):
    return jax.shard_map(
        shards,
        mesh=mesh,
        in_specs=(
            P(None, None, "lat", "lon"),
            P(None, None, "lat", "lon"),
            P(None, "lat", "lon"),
            P(None, "lat", "lon"),
            P(None, "lat", "lon"),
            P(None, "lat", "lon"),
            P(None, "lat", "lon"),
            P("lat", "lon"),
            P("lat", "lon"),
            P(None, "lat", "lon"),
            P(),
        ),
        out_specs=(P(None, None, "lat", "lon"), P(None, "lat", "lon"), P(None, "lat", "lon")),
        check_vma=False,
    )
```

```python
import jax
import jax.numpy as jnp
from jax import lax
from jax.experimental import pallas as pl
from jax.experimental.pallas import tpu as pltpu
from jax.sharding import PartitionSpec as P

COURANT = 0.3
TIME_STEP = 0.25

N = 128
BINS = 4
MAIN = 2 * BINS + 3
EXTRA = BINS + 1
EAST, NORTH, RHO = 2 * BINS, 2 * BINS + 1, 2 * BINS + 2
LINES = 4 * MAIN + 2 * EXTRA
LAT_MSG = 56
LON_MSG = 56
BASE = 16
ROWS = 160
OWN_FLOPS = 3_000_000
OWN_TALL, FIRST_TALL = 48, 48
REST_TALL, REST_END = 24, 32
EARLY = 10
EDGE_TALL, EDGE_END = 144, 128
PLANES = MAIN + EXTRA + 1
GROUND = MAIN + EXTRA
F32 = jnp.float32


def position():
    lat, lon = lax.axis_index("lat"), lax.axis_index("lon")
    last = lax.axis_size("lat") - 1
    return lat % 2, lon % 2, (lat == 0).astype(jnp.int32), (lat == last).astype(jnp.int32)


def plane_readers(refs, info):
    tracer, adjoint, speed_e, speed_n, sign_e, sign_n, density, land, mask, emission = refs

    def east(at, size):
        s = speed_e[0, pl.ds(at, size), :]
        return jnp.where(sign_e[0, pl.ds(at, size), :] == 1, s, -s)

    def north(at, size):
        s = speed_n[0, pl.ds(at, size), :]
        s = jnp.where(sign_n[0, pl.ds(at, size), :] == 1, s, -s)
        row = lax.broadcasted_iota(jnp.int32, (size, N), 0) + at
        return jnp.where((row == 0) & (info[2] == 1), 0.0, s)

    def source(b):
        def read(at, size):
            m = mask[pl.ds(at, size), :].astype(F32)
            return TIME_STEP * m * emission[b, pl.ds(at, size), :]

        return read

    main = [lambda at, size, b=b: tracer[b, 0, pl.ds(at, size), :] for b in range(BINS)]
    main += [lambda at, size, b=b: adjoint[b, 0, pl.ds(at, size), :] for b in range(BINS)]
    main += [east, north, lambda at, size: density[0, pl.ds(at, size), :]]
    extra = [source(b) for b in range(BINS)]
    extra += [lambda at, size: land[pl.ds(at, size), :].astype(F32)]
    return main, extra


def pack_kernel(*refs):
    info = position()
    sources, (out0, out1, lines_out, planes), ins = refs[:10], refs[10:14], refs[14:24]
    edge, packed, sem = refs[24:]
    copies = [pltpu.make_async_copy(x, y, sem.at[i]) for i, (x, y) in enumerate(zip(sources, ins, strict=True))]
    for copy in copies:
        copy.start()
    for copy in copies:
        copy.wait()
    main, extra = plane_readers(ins, info)
    lane = lax.broadcasted_iota(jnp.int32, (N, N), 1)
    for p, read in enumerate(main + extra):
        planes[p] = read(0, N)
    planes[GROUND] = TIME_STEP * ins[8][...].astype(F32)
    for p in range(MAIN):
        edge[0, 4 * p : 4 * p + 4, :] = planes[p, 0:4, :]
        edge[1, 4 * p : 4 * p + 4, :] = planes[p, N - 4 :, :]
    for q in range(EXTRA):
        at = 4 * MAIN + 2 * q
        edge[0, at : at + 2, :] = planes[MAIN + q, 0:2, :]
        edge[1, at : at + 2, :] = planes[MAIN + q, N - 2 :, :]
    edge[:, LINES:LAT_MSG, :] = jnp.zeros((2, LAT_MSG - LINES, N), F32)
    parity = info[0]
    out0[...] = edge[1 - parity]
    out1[...] = edge[parity]
    both = jnp.zeros((N, N), F32)
    for p in range(MAIN):
        turned = pltpu.roll(planes[p], 8 * p + 4, 1)
        both = jnp.where((lane >= 8 * p) & (lane < 8 * p + 8), turned, both)
    for q in range(EXTRA):
        at = 8 * MAIN + 4 * q
        turned = pltpu.roll(planes[MAIN + q], at + 2, 1)
        both = jnp.where((lane >= at) & (lane < at + 4), turned, both)
    packed[...] = both.T
    for p in range(MAIN):
        lines_out[1, 4 * p : 4 * p + 4, :] = packed[8 * p : 8 * p + 4, :]
        lines_out[0, 4 * p : 4 * p + 4, :] = packed[8 * p + 4 : 8 * p + 8, :]
    for q in range(EXTRA):
        at, to = 8 * MAIN + 4 * q, 4 * MAIN + 2 * q
        lines_out[1, to : to + 2, :] = packed[at : at + 2, :]
        lines_out[0, to : to + 2, :] = packed[at + 2 : at + 4, :]
    lines_out[:, LINES:LON_MSG, :] = jnp.zeros((2, LON_MSG - LINES, N), F32)


def place_lat(info, got0, got1, halo):
    parity = info[0]
    halo[1 - parity] = got0[1 - parity]
    halo[parity] = got1[...]
    at = 4 * RHO

    @pl.when(info[2] == 1)
    def _():
        halo[0, at : at + 4, :] = jnp.ones((4, N), F32)

    @pl.when(info[3] == 1)
    def _():
        halo[1, at : at + 4, :] = jnp.ones((4, N), F32)


def corner_kernel(got1, got0, lines, out, halo, rows):
    info = position()
    place_lat(info, got0, got1, halo)
    rows[8 * MAIN :, :] = jnp.zeros((N - 8 * MAIN, N), F32)
    for p in range(MAIN):
        rows[8 * p : 8 * p + 4, :] = halo[0, 4 * p : 4 * p + 4, :]
        rows[8 * p + 4 : 8 * p + 8, :] = halo[1, 4 * p : 4 * p + 4, :]
    turned = rows[...].T
    parity = info[1]
    out[0:LON_MSG, :] = lines[1 - parity]
    out[LON_MSG:, :] = lines[parity]
    left, right = turned[0:8][:2], turned[N - 8 :][6:]

    @pl.when(parity == 0)
    def _():
        out[LINES : LON_MSG, :] = right
        out[LON_MSG + LINES : 2 * LON_MSG, :] = left

    @pl.when(parity == 1)
    def _():
        out[LINES : LON_MSG, :] = left
        out[LON_MSG + LINES : 2 * LON_MSG, :] = right


def shift(x, s):
    return pltpu.roll(x, (-s) % N, 1)


def face(blows, c2, c1, c0, cp):
    near_up = jnp.where(blows, c1, c0)
    far_up = jnp.where(blows, c2, cp)
    return 2.0 * (c0 + c1) + 3.0 * near_up - far_up


def spread_east(blows, grads):
    plus = jnp.where(blows, grads, 0.0)
    minus = grads - plus
    twice = 2.0 * grads
    after = twice + 3.0 * plus - shift(plus, 1)
    before = twice + 3.0 * minus - shift(minus, -1)
    return shift(after, 1) + before


def spread_north(winds, grads):
    total = 2.0 * (grads[1] + grads[2])
    total += 3.0 * (jnp.where(winds[2], grads[2], 0.0) + jnp.where(winds[1], 0.0, grads[1]))
    return total - jnp.where(winds[3], grads[3], 0.0) - jnp.where(winds[0], 0.0, grads[0])


def lay(sizes):
    at, total = {}, 0
    for name, size in sizes:
        at[name] = total
        total += size
    return at, total


def places(count):
    return lay((("mass", 2), ("scale", 1), ("keep", count), ("g", count)))


def results(count):
    return lay((("middle", count), ("seen", count), ("gm", count), ("flux", 2 * count)))


def prepare_half(tall, count, field_of, keep_of, state):
    field = field_of(tall)
    at, _ = places(count)

    def put(name, b, row, value):
        state[at[name] + b, pl.ds(row, tall), :] = value

    def prepare(t, carry):
        row = pl.multiple_of(8 + t * tall, 8)
        rho = field("rho", 0, row)
        put("mass", 0, row, field("east", 0, row) * (rho + shift(rho, -1)) * (1.0 / 12.0))
        put("mass", 1, row, field("north", 0, row) * (rho + field("rho", 0, row - 1)) * (1.0 / 12.0))
        scale = COURANT / rho
        put("scale", 0, row, scale)
        for b, kept in enumerate(keep_of(row)):
            put("g", b, row, field("adjoint", b, row) * scale)
            put("keep", b, row, kept)
        return carry

    lax.fori_loop(0, 144 // tall, prepare, 0)


def first_half(tall, count, field_of, start, state, back):
    field = field_of(tall)
    at, _ = places(count)
    to, _ = results(count)

    def get(name, b, row):
        if name in at:
            return start[at[name] + b, pl.ds(row, tall), :]
        return state[to[name] + b, pl.ds(row, tall), :]

    def put(name, b, row, value):
        state[to[name] + b, pl.ds(row, tall), :] = value

    def first(t, carry):
        row = pl.multiple_of(8 + t * tall, 8)
        blows_e, blows_n = field("east", 0, row) > 0.0, field("north", 0, row) > 0.0
        mass_e, mass_n, scale = get("mass", 0, row), get("mass", 1, row), get("scale", 0, row)
        for b in range(count):
            c, kept = field("tracer", b, row), get("keep", b, row)
            fe = mass_e * face(blows_e, shift(c, -2), shift(c, -1), c, shift(c, 1))
            fn = mass_n * face(
                blows_n, field("tracer", b, row - 2), field("tracer", b, row - 1), c, field("tracer", b, row + 1)
            )
            put("flux", b, row, fe)
            put("flux", count + b, row, fn)
            put("middle", b, row, c * kept + field("source", b, row) - scale * (shift(fe, 1) - fe))
            gb = get("g", b, row)
            back[b, pl.ds(row, tall), :] = mass_n * (gb - get("g", b, row - 1))
            ge = mass_e * (gb - shift(gb, -1))
            put("seen", b, row, field("adjoint", b, row) * kept + spread_east(blows_e, ge))
        return carry

    lax.fori_loop(0, 144 // tall, first, 0)

    def join(t, carry):
        row = pl.multiple_of(8 + t * tall, 8)
        winds = [field("north", 0, row + dr) > 0.0 for dr in (-1, 0, 1, 2)]
        scale = get("scale", 0, row)
        for b in range(count):
            change = get("flux", count + b, row + 1) - get("flux", count + b, row)
            put("middle", b, row, get("middle", b, row) - scale * change)
            whole = get("seen", b, row) + spread_north(winds, [back[b, pl.ds(row + dr, tall), :] for dr in (-1, 0, 1, 2)])
            put("seen", b, row, whole)
            put("gm", b, row, whole * scale)
        return carry

    lax.fori_loop(0, 144 // tall, join, 0)


def second_half(tall, end_tall, count, field_of, start, state, flux2, bank, part, rim, give):
    at, _ = places(count)
    to, _ = results(count)
    field = field_of(tall)

    def get(name, b, row, size=tall):
        if name in at:
            return start[at[name] + b, pl.ds(row, size), :]
        return state[to[name] + b, pl.ds(row, size), :]

    def last(t, carry):
        row = pl.multiple_of(8 + t * tall, 8)
        blows_e, blows_n = field("east", 0, row) > 0.0, field("north", 0, row) > 0.0
        mass_e, mass_n = get("mass", 0, row), get("mass", 1, row)
        rho = field("rho", 0, row)
        rim_e = rim_n = own = jnp.zeros((tall, N), F32)
        for b in range(count):
            c = get("middle", b, row)
            fe = mass_e * face(blows_e, shift(c, -2), shift(c, -1), c, shift(c, 1))
            fn = mass_n * face(blows_n, get("middle", b, row - 2), get("middle", b, row - 1), c, get("middle", b, row + 1))
            flux2[b, pl.ds(row, tall), :] = fn
            ga, gb = get("g", b, row), get("gm", b, row)
            old, old_n = get("flux", b, row), get("flux", count + b, row)
            deb = gb - shift(gb, -1)
            dnb = gb - get("gm", b, row - 1)
            rim_e += fe * (ga - shift(ga, -1)) + old * deb
            rim_n += fn * (ga - get("g", b, row - 1)) + old_n * dnb
            own += ga * (shift(fe, 1) - fe) + gb * (shift(old, 1) - old)
            bank[b, pl.ds(row, tall), :] = mass_n * dnb
            part[b, pl.ds(row, tall), :] = get("seen", b, row) * get("keep", b, row) + spread_east(blows_e, mass_e * deb)
        rim_e = rim_e / (rho + shift(rho, -1))
        rim[0, pl.ds(row, tall), :] = rim_n / (rho + field("rho", 0, row - 1))
        rim[1, pl.ds(row, tall), :] = own
        rim[2, pl.ds(row, tall), :] = rim_e + shift(rim_e, 1)
        return carry

    lax.fori_loop(0, 144 // tall, last, 0)

    def finish(t, carry):
        row = pl.multiple_of(BASE + t * end_tall, 8)
        field = field_of(end_tall)
        winds = [field("north", 0, row + dr) > 0.0 for dr in (-1, 0, 1, 2)]
        own = rim[1, pl.ds(row, end_tall), :]
        adjoints = []
        for b in range(count):
            grads = [bank[b, pl.ds(row + dr, end_tall), :] for dr in (-1, 0, 1, 2)]
            adjoints.append(part[b, pl.ds(row, end_tall), :] + spread_north(winds, grads))
            own += get("g", b, row, end_tall) * (flux2[b, pl.ds(row + 1, end_tall), :] - flux2[b, pl.ds(row, end_tall), :])
            own += get("gm", b, row, end_tall) * (get("flux", count + b, row + 1, end_tall) - get("flux", count + b, row, end_tall))
        total = own / field("rho", 0, row) + rim[2, pl.ds(row, end_tall), :] + rim[0, pl.ds(row, end_tall), :]
        seen = [field("adjoint", b, row) + get("seen", b, row, end_tall) for b in range(count)]
        give(row, pl.multiple_of(t * end_tall, 8), adjoints, total + rim[0, pl.ds(row + 1, end_tall), :], seen)
        return carry

    lax.fori_loop(0, N // end_tall, finish, 0)


PLACE = {"tracer": 0, "adjoint": BINS, "east": EAST, "north": NORTH, "rho": RHO, "source": MAIN, "land": MAIN + BINS}


def block_field(planes):
    return lambda tall: lambda name, b, row: planes[PLACE[name] + b, pl.ds(row, tall), :]


STRIPS = ("tracer", "adjoint", "source", "east", "north", "rho", "land")


def strip_field(strips):
    return lambda tall: lambda name, b, row: strips[STRIPS.index(name), pl.ds(row, tall), :]


def own_kernel(deposition, *refs):
    info = position()
    block, got0, got1, _, planes, start, strips, rates, *outs, halo = refs[:12]
    work = refs[12:]
    place_lat(info, got0, got1, halo)
    for p in range(MAIN):
        planes[p, BASE : BASE + N, :] = block[p]
        planes[p, BASE - 4 : BASE, :] = halo[0, 4 * p : 4 * p + 4, :]
        planes[p, BASE + N : BASE + N + 4, :] = halo[1, 4 * p : 4 * p + 4, :]
    for q in range(EXTRA):
        at, p = 4 * MAIN + 2 * q, MAIN + q
        planes[p, BASE : BASE + N, :] = block[p]
        planes[p, BASE - 2 : BASE, :] = halo[0, at : at + 2, :]
        planes[p, BASE + N : BASE + N + 2, :] = halo[1, at : at + 2, :]
    field = block_field(planes)(OWN_TALL)

    def keep_of(row):
        land = field("land", 0, row)
        for b in range(BINS):
            rate = jnp.zeros_like(land)
            for kind in range(8):
                rate = jnp.where(land == float(kind), deposition[b, kind], rate)
            yield 1.0 - TIME_STEP * rate

    prepare_half(OWN_TALL, BINS, block_field(planes), keep_of, start)
    lane = lax.broadcasted_iota(jnp.int32, (OWN_TALL, N), 1)

    bins = lax.broadcasted_iota(jnp.int32, (1, N), 1) // 32
    for kind in range(8):
        rate = jnp.where(bins == 0, deposition[0, kind], deposition[1, kind])
        rate = jnp.where(bins < 2, rate, jnp.where(bins == 2, deposition[2, kind], deposition[3, kind]))
        rates[kind : kind + 1, :] = rate

    def cut(t, carry):
        row = pl.multiple_of(8 + t * OWN_TALL, 8)
        for i, name in enumerate(STRIPS):
            if name in ("tracer", "adjoint", "source"):
                both = jnp.zeros((OWN_TALL, N), F32)
                for b in range(BINS):
                    x, low = field(name, b, row), 32 * b
                    both = jnp.where((lane >= low) & (lane < low + 12), pltpu.roll(x, (low + 12) % N, 1), both)
                    both = jnp.where((lane >= low + 20) & (lane < low + 32), pltpu.roll(x, (low + 20) % N, 1), both)
            else:
                x = field(name, 0, row)
                both = jnp.where(lane < 12, pltpu.roll(x, 12, 1), 0.0)
                both = jnp.where((lane >= 20) & (lane < 32), pltpu.roll(x, 20, 1), both)
                both = jnp.where(lane % 64 < 32, both, pltpu.roll(both, 32, 1))
                both = jnp.where(lane < 64, both, pltpu.roll(both, 64, 1))
            strips[i, pl.ds(row, OWN_TALL), :] = both
        return carry

    lax.fori_loop(0, 144 // OWN_TALL, cut, 0)

    @pl.when(runs_early())
    def _():
        both_halves(planes, start, block, outs, work)


def runs_early():
    return (lax.axis_index("lon") % 2 == 1) | (lax.axis_index("lat") >= EARLY * lax.axis_size("lat") // 16)


def both_halves(planes, start, block, outs, work):
    adj_out, dens_out, emis_out = outs
    state, back, flux2, bank, part, rim = work
    first_half(FIRST_TALL, BINS, block_field(planes), start, state, back)

    def give(row, at, adjoints, dens, seen):
        ground = block[GROUND, pl.ds(at, REST_END), :]
        for b in range(BINS):
            adj_out[b, 0, pl.ds(at, REST_END), :] = adjoints[b]
            emis_out[b, pl.ds(at, REST_END), :] = ground * seen[b]
        dens_out[0, pl.ds(at, REST_END), :] = dens

    second_half(REST_TALL, REST_END, BINS, block_field(planes), start, state, flux2, bank, part, rim, give)


def rest_kernel(planes, start, block, near, *refs):
    del near

    @pl.when(jnp.logical_not(runs_early()))
    def _():
        both_halves(planes, start, block, refs[3:6], refs[6:])


def edge_kernel(rates, strips_in, near, passed, adj, dens, emis, block, *refs):
    adj_out, dens_out, emis_out, strips, sides, turn, start, state, back, flux2, bank, part, rim = refs
    lane = lax.broadcasted_iota(jnp.int32, (8, N), 1)
    parity = position()[1]
    sides[1 - parity] = near[0:LON_MSG, :]
    sides[parity] = passed[...]
    tall = lax.broadcasted_iota(jnp.int32, (N, N), 1) % 32
    strips[:, 8:BASE, :] = strips_in[:, 8:BASE, :]
    strips[:, BASE + N : BASE + N + 8, :] = strips_in[:, BASE + N : BASE + N + 8, :]
    for i, name in enumerate(STRIPS):
        wide = 2 if name in ("source", "land") else 4
        inside = (tall >= 16 - wide - (4 - wide)) & (tall < 12 + wide) | (tall >= 20 - wide) & (tall < 20)
        for b in range(BINS):
            p = PLACE[name] + (b if name in ("tracer", "adjoint", "source") else 0)
            at = 4 * p if p < MAIN else 4 * MAIN + 2 * (p - MAIN)
            turn[i, 32 * b + 12 : 32 * b + 12 + wide, :] = sides[1, at : at + wide, :]
            turn[i, 32 * b + 20 - wide : 32 * b + 20, :] = sides[0, at : at + wide, :]
        strips[i, BASE : BASE + N, :] = jnp.where(inside, turn[i].T, strips_in[i, BASE : BASE + N, :])
    turn[0, 0:2, :] = sides[1, LINES:LON_MSG, :]
    turn[0, 6:8, :] = sides[0, LINES:LON_MSG, :]
    turned = turn[0].T
    for i, name in enumerate(STRIPS):
        if name in ("source", "land"):
            continue
        low, high = strips[i, BASE - 8 : BASE, :], strips[i, BASE + N : BASE + N + 8, :]
        sub = lax.broadcasted_iota(jnp.int32, (8, N), 0)
        for b in range(BINS):
            p = PLACE[name] + (b if name in ("tracer", "adjoint") else 0)
            eight = pltpu.roll(turned[8 * p : 8 * p + 8], 32 * b + 12, 1)
            inside = (lane >= 32 * b + 12) & (lane < 32 * b + 20)
            half = pltpu.roll(eight, 4, 0)
            low = jnp.where(inside & (sub >= 4), half, low)
            high = jnp.where(inside & (sub < 4), half, high)
        strips[i, BASE - 8 : BASE, :] = low
        strips[i, BASE + N : BASE + N + 8, :] = high
    field = strip_field(strips)(EDGE_TALL)
    def keep_of(row):
        land = field("land", 0, row)
        rate = jnp.zeros_like(land)
        for kind in range(8):
            rate = jnp.where(land == float(kind), rates[kind : kind + 1, :], rate)
        yield 1.0 - TIME_STEP * rate

    prepare_half(EDGE_TALL, 1, strip_field(strips), keep_of, start)
    first_half(EDGE_TALL, 1, strip_field(strips), start, state, back)
    lane = lax.broadcasted_iota(jnp.int32, (EDGE_END, N), 1)
    left, right = lane < 4, lane >= N - 4

    def patch(value, b, old):
        value_right = pltpu.roll(value, (116 - 32 * b) % N, 1)
        value_left = pltpu.roll(value, (-32 * b - 20) % N, 1)
        return jnp.where(left, value_left, jnp.where(right, value_right, old))

    def give(row, at, adjoints, total, seen):
        ground = block[GROUND, pl.ds(at, EDGE_END), :]
        for b in range(BINS):
            adj_out[b, 0, pl.ds(at, EDGE_END), :] = patch(adjoints[0], b, adj[b, 0, pl.ds(at, EDGE_END), :])
            old = emis[b, pl.ds(at, EDGE_END), :]
            emis_out[b, pl.ds(at, EDGE_END), :] = jnp.where(left | right, ground * patch(seen[0], b, old), old)
        total = total + pltpu.roll(total, 32, 1)
        total = total + pltpu.roll(total, 64, 1)
        dens_out[0, pl.ds(at, EDGE_END), :] = patch(total, 0, dens[0, pl.ds(at, EDGE_END), :])

    second_half(EDGE_TALL, EDGE_END, 1, strip_field(strips), start, state, flux2, bank, part, rim, give)


def swaps(count, offset, closed):
    pairs = []
    for low in range(offset, count, 2):
        high = low + 1
        if high >= count and closed:
            continue
        pairs += [(low, high % count), (high % count, low)]
    return pairs


SMEM = pl.BlockSpec(memory_space=pltpu.SMEM)
VMEM = pl.BlockSpec(memory_space=pltpu.VMEM)
HBM = pl.BlockSpec(memory_space=pltpu.HBM)


def kernel_call(body, smem, arrays, out_shapes, scratch, place=VMEM, extra=(), flops=0, fast=True, aliases=None):
    return pl.pallas_call(
        body,
        out_shape=[pltpu.VMEM(s, F32) if fast else jax.ShapeDtypeStruct(s, F32) for s in out_shapes],
        in_specs=[SMEM] * smem + [place] * (len(arrays) - smem),
        out_specs=[VMEM] * len(out_shapes),
        scratch_shapes=[pltpu.VMEM(s, F32) for s in scratch] + list(extra),
        input_output_aliases=aliases or {},
        compiler_params=pltpu.CompilerParams(vmem_limit_bytes=24 * 1024 * 1024),
        cost_estimate=pl.CostEstimate(flops=flops, bytes_accessed=0, transcendentals=0) if flops else None,
    )(*arrays)


def shards(*args):
    ins, deposition = args[:10], args[10].T
    lats, lons = lax.axis_size("lat"), lax.axis_size("lon")
    msg = (LAT_MSG, N)
    ins = [pltpu.with_memory_space_constraint(x, pltpu.HBM) for x in ins]
    out0, out1, lines, block = kernel_call(
        pack_kernel,
        0,
        ins,
        [msg, msg, (2, LON_MSG, N), (PLANES, N, N)],
        [],
        HBM,
        [pltpu.VMEM(x.shape, x.dtype) for x in ins]
        + [pltpu.VMEM((2, *msg), F32), pltpu.VMEM((N, N), F32), pltpu.SemaphoreType.DMA((10,))],
    )
    got1 = lax.ppermute(out1, "lat", swaps(lats, 1, True))
    got0 = lax.all_gather(out0, "lat", axis_index_groups=[[i, i + 1] for i in range(0, lats, 2)])
    (both,) = kernel_call(corner_kernel, 0, (got1, got0, lines), [(2 * LON_MSG, N)], [(2, *msg), (N, N)])
    near = lax.ppermute(both, "lon", swaps(lons, 0, False))
    plane = (ROWS, N)
    shapes = [(BINS, 1, N, N), (1, N, N), (BINS, N, N)]
    work = [(results(BINS)[1], *plane)] + [(BINS, *plane)] * 4 + [(3, *plane)]
    planes, start, strips, rates, *first_outs = kernel_call(
        own_kernel,
        1,
        (deposition, block, got0, got1, both),
        [(MAIN + EXTRA, *plane), (places(BINS)[1], *plane), (len(STRIPS), *plane), (8, N), *shapes],
        [(2, *msg), *work],
        flops=OWN_FLOPS,
    )
    onward = [(i, (i + (2 if i % 2 == 0 else lons - 2)) % lons) for i in range(lons)]
    near, strips = lax.optimization_barrier((near, strips))
    passed = lax.ppermute(near[LON_MSG:], "lon", onward)
    adj, dens, emis = kernel_call(
        rest_kernel,
        0,
        (planes, start, block, near, *first_outs),
        shapes,
        work,
        aliases={4: 0, 5: 1, 6: 2},
        flops=OWN_FLOPS,
    )
    outs = kernel_call(
        edge_kernel,
        0,
        (rates, strips, near, passed, adj, dens, emis, block),
        shapes,
        [
            (len(STRIPS), *plane),
            (2, LON_MSG, N),
            (len(STRIPS), N, N),
            (places(1)[1], *plane),
            (results(1)[1], *plane),
            (1, *plane),
            (1, *plane),
            (1, *plane),
            (1, *plane),
            (3, *plane),
        ],
        fast=False,
    )
    return tuple(outs)


def solution(mesh):
    return jax.shard_map(
        shards,
        mesh=mesh,
        in_specs=(
            P(None, None, "lat", "lon"),
            P(None, None, "lat", "lon"),
            P(None, "lat", "lon"),
            P(None, "lat", "lon"),
            P(None, "lat", "lon"),
            P(None, "lat", "lon"),
            P(None, "lat", "lon"),
            P("lat", "lon"),
            P("lat", "lon"),
            P(None, "lat", "lon"),
            P(),
        ),
        out_specs=(P(None, None, "lat", "lon"), P(None, "lat", "lon"), P(None, "lat", "lon")),
        check_vma=False,
    )
```

```python
import jax
import jax.numpy as jnp
from jax import lax
from jax.experimental import pallas as pl
from jax.experimental.pallas import tpu as pltpu
from jax.sharding import PartitionSpec as P

COURANT = 0.3
TIME_STEP = 0.25

N = 128
BINS = 4
MAIN = 2 * BINS + 3
EXTRA = BINS + 1
EAST, NORTH, RHO = 2 * BINS, 2 * BINS + 1, 2 * BINS + 2
LINES = 4 * MAIN + 2 * EXTRA
LAT_MSG = 56
LON_MSG = 56
BASE = 16
ROWS = 160
OWN_FLOPS = 3_000_000
OWN_TALL, FIRST_TALL = 48, 48
REST_TALL, REST_END = 24, 32
EARLY = 10
EDGE_TALL, EDGE_END = 144, 128
F32 = jnp.float32


def position():
    lat, lon = lax.axis_index("lat"), lax.axis_index("lon")
    last = lax.axis_size("lat") - 1
    return lat % 2, lon % 2, (lat == 0).astype(jnp.int32), (lat == last).astype(jnp.int32)


def block_planes(tracer, adjoint, emission, few):
    planes = [tracer[b, 0] for b in range(BINS)] + [adjoint[b, 0] for b in range(BINS)]
    planes += [few[i] for i in range(3)] + [few[4] * emission[b] for b in range(BINS)]
    return [*planes, few[3]]


def rows_kernel(*refs):
    large, small, (out0, out1, few) = refs[:3], refs[3:10], refs[10:13]
    tiles, (speed_e, speed_n, sign_e, sign_n, land, mask), (edge, sem) = refs[13:16], refs[16:22], refs[22:]
    info = position()
    whole = [speed_e, speed_n, sign_e, sign_n, few.at[pl.ds(2, 1)], land, mask]
    copies = [pltpu.make_async_copy(x, y, sem.at[i]) for i, (x, y) in enumerate(zip(small, whole, strict=True))]
    for i, (x, y) in enumerate(zip(large, tiles, strict=True)):
        x = x.at[:, 0] if i < 2 else x
        for side, at in enumerate((0, N - 8)):
            copies.append(pltpu.make_async_copy(x.at[:, pl.ds(at, 8)], y.at[side], sem.at[7 + 2 * i + side]))
    for copy in copies:
        copy.start()
    for copy in copies:
        copy.wait()
    row = lax.broadcasted_iota(jnp.int32, (N, N), 0)
    few[0] = jnp.where(sign_e[0] == 1, speed_e[0], -speed_e[0])
    wind = jnp.where(sign_n[0] == 1, speed_n[0], -speed_n[0])
    few[1] = jnp.where((row == 0) & (info[2] == 1), 0.0, wind)
    few[3] = land[...].astype(F32)
    few[4] = TIME_STEP * mask[...].astype(F32)
    tracer, adjoint, emission = tiles
    for side, at in enumerate((0, N - 8)):
        low, high = (0, 4) if side == 0 else (4, 8)
        main = [tracer[side, b] for b in range(BINS)] + [adjoint[side, b] for b in range(BINS)]
        for p, value in enumerate(main + [few[i, at : at + 8, :] for i in range(3)]):
            edge[side, 4 * p : 4 * p + 4, :] = value[low:high]
        ground = few[4, at : at + 8, :]
        extra = [ground * emission[side, b] for b in range(BINS)] + [few[3, at : at + 8, :]]
        low, high = (0, 2) if side == 0 else (6, 8)
        for q, value in enumerate(extra):
            to = 4 * MAIN + 2 * q
            edge[side, to : to + 2, :] = value[low:high]
    edge[:, LINES:LAT_MSG, :] = jnp.zeros((2, LAT_MSG - LINES, N), F32)
    parity = info[0]
    out0[...] = edge[1 - parity]
    out1[...] = edge[parity]


def pack_kernel(*refs):
    tracer, adjoint, emission, few, _, lines_out, packed = refs
    lane = lax.broadcasted_iota(jnp.int32, (N, N), 1)
    planes = block_planes(tracer, adjoint, emission, few)
    both = jnp.zeros((N, N), F32)
    for p in range(MAIN):
        turned = pltpu.roll(planes[p], 8 * p + 4, 1)
        both = jnp.where((lane >= 8 * p) & (lane < 8 * p + 8), turned, both)
    for q in range(EXTRA):
        at = 8 * MAIN + 4 * q
        turned = pltpu.roll(planes[MAIN + q], at + 2, 1)
        both = jnp.where((lane >= at) & (lane < at + 4), turned, both)
    packed[...] = both.T
    for p in range(MAIN):
        lines_out[1, 4 * p : 4 * p + 4, :] = packed[8 * p : 8 * p + 4, :]
        lines_out[0, 4 * p : 4 * p + 4, :] = packed[8 * p + 4 : 8 * p + 8, :]
    for q in range(EXTRA):
        at, to = 8 * MAIN + 4 * q, 4 * MAIN + 2 * q
        lines_out[1, to : to + 2, :] = packed[at : at + 2, :]
        lines_out[0, to : to + 2, :] = packed[at + 2 : at + 4, :]
    lines_out[:, LINES:LON_MSG, :] = jnp.zeros((2, LON_MSG - LINES, N), F32)


def place_lat(info, got0, got1, halo):
    parity = info[0]
    halo[1 - parity] = got0[1 - parity]
    halo[parity] = got1[...]
    at = 4 * RHO

    @pl.when(info[2] == 1)
    def _():
        halo[0, at : at + 4, :] = jnp.ones((4, N), F32)

    @pl.when(info[3] == 1)
    def _():
        halo[1, at : at + 4, :] = jnp.ones((4, N), F32)


def corner_kernel(got1, got0, lines, out, halo, rows):
    info = position()
    place_lat(info, got0, got1, halo)
    rows[8 * MAIN :, :] = jnp.zeros((N - 8 * MAIN, N), F32)
    for p in range(MAIN):
        rows[8 * p : 8 * p + 4, :] = halo[0, 4 * p : 4 * p + 4, :]
        rows[8 * p + 4 : 8 * p + 8, :] = halo[1, 4 * p : 4 * p + 4, :]
    turned = rows[...].T
    parity = info[1]
    out[0:LON_MSG, :] = lines[1 - parity]
    out[LON_MSG:, :] = lines[parity]
    left, right = turned[0:8][:2], turned[N - 8 :][6:]

    @pl.when(parity == 0)
    def _():
        out[LINES : LON_MSG, :] = right
        out[LON_MSG + LINES : 2 * LON_MSG, :] = left

    @pl.when(parity == 1)
    def _():
        out[LINES : LON_MSG, :] = left
        out[LON_MSG + LINES : 2 * LON_MSG, :] = right


def shift(x, s):
    return pltpu.roll(x, (-s) % N, 1)


def face(blows, c2, c1, c0, cp):
    near_up = jnp.where(blows, c1, c0)
    far_up = jnp.where(blows, c2, cp)
    return 2.0 * (c0 + c1) + 3.0 * near_up - far_up


def spread_east(blows, grads):
    plus = jnp.where(blows, grads, 0.0)
    minus = grads - plus
    twice = 2.0 * grads
    after = twice + 3.0 * plus - shift(plus, 1)
    before = twice + 3.0 * minus - shift(minus, -1)
    return shift(after, 1) + before


def spread_north(winds, grads):
    total = 2.0 * (grads[1] + grads[2])
    total += 3.0 * (jnp.where(winds[2], grads[2], 0.0) + jnp.where(winds[1], 0.0, grads[1]))
    return total - jnp.where(winds[3], grads[3], 0.0) - jnp.where(winds[0], 0.0, grads[0])


def lay(sizes):
    at, total = {}, 0
    for name, size in sizes:
        at[name] = total
        total += size
    return at, total


def places(count):
    return lay((("mass", 2), ("scale", 1), ("keep", count), ("g", count)))


def results(count):
    return lay((("middle", count), ("seen", count), ("gm", count), ("flux", 2 * count)))


def prepare_half(tall, count, field_of, keep_of, state):
    field = field_of(tall)
    at, _ = places(count)

    def put(name, b, row, value):
        state[at[name] + b, pl.ds(row, tall), :] = value

    def prepare(t, carry):
        row = pl.multiple_of(8 + t * tall, 8)
        rho = field("rho", 0, row)
        put("mass", 0, row, field("east", 0, row) * (rho + shift(rho, -1)) * (1.0 / 12.0))
        put("mass", 1, row, field("north", 0, row) * (rho + field("rho", 0, row - 1)) * (1.0 / 12.0))
        scale = COURANT / rho
        put("scale", 0, row, scale)
        for b, kept in enumerate(keep_of(row)):
            put("g", b, row, field("adjoint", b, row) * scale)
            put("keep", b, row, kept)
        return carry

    lax.fori_loop(0, 144 // tall, prepare, 0)


def first_half(tall, count, field_of, start, state, back):
    field = field_of(tall)
    at, _ = places(count)
    to, _ = results(count)

    def get(name, b, row):
        if name in at:
            return start[at[name] + b, pl.ds(row, tall), :]
        return state[to[name] + b, pl.ds(row, tall), :]

    def put(name, b, row, value):
        state[to[name] + b, pl.ds(row, tall), :] = value

    def first(t, carry):
        row = pl.multiple_of(8 + t * tall, 8)
        blows_e, blows_n = field("east", 0, row) > 0.0, field("north", 0, row) > 0.0
        mass_e, mass_n, scale = get("mass", 0, row), get("mass", 1, row), get("scale", 0, row)
        for b in range(count):
            c, kept = field("tracer", b, row), get("keep", b, row)
            fe = mass_e * face(blows_e, shift(c, -2), shift(c, -1), c, shift(c, 1))
            fn = mass_n * face(
                blows_n, field("tracer", b, row - 2), field("tracer", b, row - 1), c, field("tracer", b, row + 1)
            )
            put("flux", b, row, fe)
            put("flux", count + b, row, fn)
            put("middle", b, row, c * kept + field("source", b, row) - scale * (shift(fe, 1) - fe))
            gb = get("g", b, row)
            back[b, pl.ds(row, tall), :] = mass_n * (gb - get("g", b, row - 1))
            ge = mass_e * (gb - shift(gb, -1))
            put("seen", b, row, field("adjoint", b, row) * kept + spread_east(blows_e, ge))
        return carry

    lax.fori_loop(0, 144 // tall, first, 0)

    def join(t, carry):
        row = pl.multiple_of(8 + t * tall, 8)
        winds = [field("north", 0, row + dr) > 0.0 for dr in (-1, 0, 1, 2)]
        scale = get("scale", 0, row)
        for b in range(count):
            change = get("flux", count + b, row + 1) - get("flux", count + b, row)
            put("middle", b, row, get("middle", b, row) - scale * change)
            whole = get("seen", b, row) + spread_north(winds, [back[b, pl.ds(row + dr, tall), :] for dr in (-1, 0, 1, 2)])
            put("seen", b, row, whole)
            put("gm", b, row, whole * scale)
        return carry

    lax.fori_loop(0, 144 // tall, join, 0)


def second_half(tall, end_tall, count, field_of, start, state, flux2, bank, part, rim, give):
    at, _ = places(count)
    to, _ = results(count)
    field = field_of(tall)

    def get(name, b, row, size=tall):
        if name in at:
            return start[at[name] + b, pl.ds(row, size), :]
        return state[to[name] + b, pl.ds(row, size), :]

    def last(t, carry):
        row = pl.multiple_of(8 + t * tall, 8)
        blows_e, blows_n = field("east", 0, row) > 0.0, field("north", 0, row) > 0.0
        mass_e, mass_n = get("mass", 0, row), get("mass", 1, row)
        rho = field("rho", 0, row)
        rim_e = rim_n = own = jnp.zeros((tall, N), F32)
        for b in range(count):
            c = get("middle", b, row)
            fe = mass_e * face(blows_e, shift(c, -2), shift(c, -1), c, shift(c, 1))
            fn = mass_n * face(blows_n, get("middle", b, row - 2), get("middle", b, row - 1), c, get("middle", b, row + 1))
            flux2[b, pl.ds(row, tall), :] = fn
            ga, gb = get("g", b, row), get("gm", b, row)
            old, old_n = get("flux", b, row), get("flux", count + b, row)
            deb = gb - shift(gb, -1)
            dnb = gb - get("gm", b, row - 1)
            rim_e += fe * (ga - shift(ga, -1)) + old * deb
            rim_n += fn * (ga - get("g", b, row - 1)) + old_n * dnb
            own += ga * (shift(fe, 1) - fe) + gb * (shift(old, 1) - old)
            bank[b, pl.ds(row, tall), :] = mass_n * dnb
            part[b, pl.ds(row, tall), :] = get("seen", b, row) * get("keep", b, row) + spread_east(blows_e, mass_e * deb)
        rim_e = rim_e / (rho + shift(rho, -1))
        rim[0, pl.ds(row, tall), :] = rim_n / (rho + field("rho", 0, row - 1))
        rim[1, pl.ds(row, tall), :] = own
        rim[2, pl.ds(row, tall), :] = rim_e + shift(rim_e, 1)
        return carry

    lax.fori_loop(0, 144 // tall, last, 0)

    def finish(t, carry):
        row = pl.multiple_of(BASE + t * end_tall, 8)
        field = field_of(end_tall)
        winds = [field("north", 0, row + dr) > 0.0 for dr in (-1, 0, 1, 2)]
        own = rim[1, pl.ds(row, end_tall), :]
        adjoints = []
        for b in range(count):
            grads = [bank[b, pl.ds(row + dr, end_tall), :] for dr in (-1, 0, 1, 2)]
            adjoints.append(part[b, pl.ds(row, end_tall), :] + spread_north(winds, grads))
            own += get("g", b, row, end_tall) * (flux2[b, pl.ds(row + 1, end_tall), :] - flux2[b, pl.ds(row, end_tall), :])
            own += get("gm", b, row, end_tall) * (get("flux", count + b, row + 1, end_tall) - get("flux", count + b, row, end_tall))
        total = own / field("rho", 0, row) + rim[2, pl.ds(row, end_tall), :] + rim[0, pl.ds(row, end_tall), :]
        seen = [field("adjoint", b, row) + get("seen", b, row, end_tall) for b in range(count)]
        give(row, pl.multiple_of(t * end_tall, 8), adjoints, total + rim[0, pl.ds(row + 1, end_tall), :], seen)
        return carry

    lax.fori_loop(0, N // end_tall, finish, 0)


PLACE = {"tracer": 0, "adjoint": BINS, "east": EAST, "north": NORTH, "rho": RHO, "source": MAIN, "land": MAIN + BINS}


def block_field(planes):
    return lambda tall: lambda name, b, row: planes[PLACE[name] + b, pl.ds(row, tall), :]


STRIPS = ("tracer", "adjoint", "source", "east", "north", "rho", "land")


def strip_field(strips):
    return lambda tall: lambda name, b, row: strips[STRIPS.index(name), pl.ds(row, tall), :]


def own_kernel(deposition, *refs):
    info = position()
    tracer, adjoint, emission, few, got0, got1, _, planes, start, strips, rates, *outs, halo = refs[:15]
    block = block_planes(tracer, adjoint, emission, few)
    work = refs[15:]
    place_lat(info, got0, got1, halo)
    for p in range(MAIN):
        planes[p, BASE : BASE + N, :] = block[p]
        planes[p, BASE - 4 : BASE, :] = halo[0, 4 * p : 4 * p + 4, :]
        planes[p, BASE + N : BASE + N + 4, :] = halo[1, 4 * p : 4 * p + 4, :]
    for q in range(EXTRA):
        at, p = 4 * MAIN + 2 * q, MAIN + q
        planes[p, BASE : BASE + N, :] = block[p]
        planes[p, BASE - 2 : BASE, :] = halo[0, at : at + 2, :]
        planes[p, BASE + N : BASE + N + 2, :] = halo[1, at : at + 2, :]
    field = block_field(planes)(OWN_TALL)

    def keep_of(row):
        land = field("land", 0, row)
        for b in range(BINS):
            rate = jnp.zeros_like(land)
            for kind in range(8):
                rate = jnp.where(land == float(kind), deposition[b, kind], rate)
            yield 1.0 - TIME_STEP * rate

    prepare_half(OWN_TALL, BINS, block_field(planes), keep_of, start)
    lane = lax.broadcasted_iota(jnp.int32, (OWN_TALL, N), 1)

    bins = lax.broadcasted_iota(jnp.int32, (1, N), 1) // 32
    for kind in range(8):
        rate = jnp.where(bins == 0, deposition[0, kind], deposition[1, kind])
        rate = jnp.where(bins < 2, rate, jnp.where(bins == 2, deposition[2, kind], deposition[3, kind]))
        rates[kind : kind + 1, :] = rate

    def cut(t, carry):
        row = pl.multiple_of(8 + t * OWN_TALL, 8)
        for i, name in enumerate(STRIPS):
            if name in ("tracer", "adjoint", "source"):
                both = jnp.zeros((OWN_TALL, N), F32)
                for b in range(BINS):
                    x, low = field(name, b, row), 32 * b
                    both = jnp.where((lane >= low) & (lane < low + 12), pltpu.roll(x, (low + 12) % N, 1), both)
                    both = jnp.where((lane >= low + 20) & (lane < low + 32), pltpu.roll(x, (low + 20) % N, 1), both)
            else:
                x = field(name, 0, row)
                both = jnp.where(lane < 12, pltpu.roll(x, 12, 1), 0.0)
                both = jnp.where((lane >= 20) & (lane < 32), pltpu.roll(x, 20, 1), both)
                both = jnp.where(lane % 64 < 32, both, pltpu.roll(both, 32, 1))
                both = jnp.where(lane < 64, both, pltpu.roll(both, 64, 1))
            strips[i, pl.ds(row, OWN_TALL), :] = both
        return carry

    lax.fori_loop(0, 144 // OWN_TALL, cut, 0)

    @pl.when(runs_early())
    def _():
        both_halves(planes, start, few, outs, work)


def runs_early():
    return (lax.axis_index("lon") % 2 == 1) | (lax.axis_index("lat") >= EARLY * lax.axis_size("lat") // 16)


def both_halves(planes, start, block, outs, work):
    adj_out, dens_out, emis_out = outs
    state, back, flux2, bank, part, rim = work
    first_half(FIRST_TALL, BINS, block_field(planes), start, state, back)

    def give(row, at, adjoints, dens, seen):
        ground = block[4, pl.ds(at, REST_END), :]
        for b in range(BINS):
            adj_out[b, 0, pl.ds(at, REST_END), :] = adjoints[b]
            emis_out[b, pl.ds(at, REST_END), :] = ground * seen[b]
        dens_out[0, pl.ds(at, REST_END), :] = dens

    second_half(REST_TALL, REST_END, BINS, block_field(planes), start, state, flux2, bank, part, rim, give)


def rest_kernel(planes, start, block, near, *refs):
    del near

    @pl.when(jnp.logical_not(runs_early()))
    def _():
        both_halves(planes, start, block, refs[3:6], refs[6:])


def edge_kernel(rates, strips_in, near, passed, adj, dens, emis, block, *refs):
    adj_out, dens_out, emis_out, strips, sides, turn, start, state, back, flux2, bank, part, rim = refs
    lane = lax.broadcasted_iota(jnp.int32, (8, N), 1)
    parity = position()[1]
    sides[1 - parity] = near[0:LON_MSG, :]
    sides[parity] = passed[...]
    tall = lax.broadcasted_iota(jnp.int32, (N, N), 1) % 32
    strips[:, 8:BASE, :] = strips_in[:, 8:BASE, :]
    strips[:, BASE + N : BASE + N + 8, :] = strips_in[:, BASE + N : BASE + N + 8, :]
    for i, name in enumerate(STRIPS):
        wide = 2 if name in ("source", "land") else 4
        inside = (tall >= 16 - wide - (4 - wide)) & (tall < 12 + wide) | (tall >= 20 - wide) & (tall < 20)
        for b in range(BINS):
            p = PLACE[name] + (b if name in ("tracer", "adjoint", "source") else 0)
            at = 4 * p if p < MAIN else 4 * MAIN + 2 * (p - MAIN)
            turn[i, 32 * b + 12 : 32 * b + 12 + wide, :] = sides[1, at : at + wide, :]
            turn[i, 32 * b + 20 - wide : 32 * b + 20, :] = sides[0, at : at + wide, :]
        strips[i, BASE : BASE + N, :] = jnp.where(inside, turn[i].T, strips_in[i, BASE : BASE + N, :])
    turn[0, 0:2, :] = sides[1, LINES:LON_MSG, :]
    turn[0, 6:8, :] = sides[0, LINES:LON_MSG, :]
    turned = turn[0].T
    for i, name in enumerate(STRIPS):
        if name in ("source", "land"):
            continue
        low, high = strips[i, BASE - 8 : BASE, :], strips[i, BASE + N : BASE + N + 8, :]
        sub = lax.broadcasted_iota(jnp.int32, (8, N), 0)
        for b in range(BINS):
            p = PLACE[name] + (b if name in ("tracer", "adjoint") else 0)
            eight = pltpu.roll(turned[8 * p : 8 * p + 8], 32 * b + 12, 1)
            inside = (lane >= 32 * b + 12) & (lane < 32 * b + 20)
            half = pltpu.roll(eight, 4, 0)
            low = jnp.where(inside & (sub >= 4), half, low)
            high = jnp.where(inside & (sub < 4), half, high)
        strips[i, BASE - 8 : BASE, :] = low
        strips[i, BASE + N : BASE + N + 8, :] = high
    field = strip_field(strips)(EDGE_TALL)
    def keep_of(row):
        land = field("land", 0, row)
        rate = jnp.zeros_like(land)
        for kind in range(8):
            rate = jnp.where(land == float(kind), rates[kind : kind + 1, :], rate)
        yield 1.0 - TIME_STEP * rate

    prepare_half(EDGE_TALL, 1, strip_field(strips), keep_of, start)
    first_half(EDGE_TALL, 1, strip_field(strips), start, state, back)
    lane = lax.broadcasted_iota(jnp.int32, (EDGE_END, N), 1)
    left, right = lane < 4, lane >= N - 4

    def patch(value, b, old):
        value_right = pltpu.roll(value, (116 - 32 * b) % N, 1)
        value_left = pltpu.roll(value, (-32 * b - 20) % N, 1)
        return jnp.where(left, value_left, jnp.where(right, value_right, old))

    def give(row, at, adjoints, total, seen):
        ground = block[4, pl.ds(at, EDGE_END), :]
        for b in range(BINS):
            adj_out[b, 0, pl.ds(at, EDGE_END), :] = patch(adjoints[0], b, adj[b, 0, pl.ds(at, EDGE_END), :])
            old = emis[b, pl.ds(at, EDGE_END), :]
            emis_out[b, pl.ds(at, EDGE_END), :] = jnp.where(left | right, ground * patch(seen[0], b, old), old)
        total = total + pltpu.roll(total, 32, 1)
        total = total + pltpu.roll(total, 64, 1)
        dens_out[0, pl.ds(at, EDGE_END), :] = patch(total, 0, dens[0, pl.ds(at, EDGE_END), :])

    second_half(EDGE_TALL, EDGE_END, 1, strip_field(strips), start, state, flux2, bank, part, rim, give)


def swaps(count, offset, closed):
    pairs = []
    for low in range(offset, count, 2):
        high = low + 1
        if high >= count and closed:
            continue
        pairs += [(low, high % count), (high % count, low)]
    return pairs


SMEM = pl.BlockSpec(memory_space=pltpu.SMEM)
VMEM = pl.BlockSpec(memory_space=pltpu.VMEM)
HBM = pl.BlockSpec(memory_space=pltpu.HBM)


def kernel_call(body, smem, arrays, out_shapes, scratch, place=VMEM, extra=(), flops=0, fast=True, aliases=None):
    return pl.pallas_call(
        body,
        out_shape=[pltpu.VMEM(s, F32) if fast else jax.ShapeDtypeStruct(s, F32) for s in out_shapes],
        in_specs=[SMEM] * smem + [place] * (len(arrays) - smem),
        out_specs=[VMEM] * len(out_shapes),
        scratch_shapes=[pltpu.VMEM(s, F32) for s in scratch] + list(extra),
        input_output_aliases=aliases or {},
        compiler_params=pltpu.CompilerParams(vmem_limit_bytes=24 * 1024 * 1024),
        cost_estimate=pl.CostEstimate(flops=flops, bytes_accessed=0, transcendentals=0) if flops else None,
    )(*arrays)


def shards(*args):
    ins, deposition = args[:10], args[10].T
    lats, lons = lax.axis_size("lat"), lax.axis_size("lon")
    msg = (LAT_MSG, N)
    large, small = [ins[0], ins[1], ins[9]], list(ins[2:9])
    out0, out1, few = kernel_call(
        rows_kernel,
        0,
        [pltpu.with_memory_space_constraint(x, pltpu.HBM) for x in large + small],
        [msg, msg, (5, N, N)],
        [],
        HBM,
        [pltpu.VMEM((2, BINS, 8, N), F32)] * 3
        + [pltpu.VMEM(x.shape, x.dtype) for i, x in enumerate(small) if i != 4]
        + [pltpu.VMEM((2, *msg), F32), pltpu.SemaphoreType.DMA((13,))],
    )
    (lines,) = kernel_call(pack_kernel, 0, (*large, few, out1), [(2, LON_MSG, N)], [(N, N)])
    got1 = lax.ppermute(out1, "lat", swaps(lats, 1, True))
    got0 = lax.all_gather(out0, "lat", axis_index_groups=[[i, i + 1] for i in range(0, lats, 2)])
    (both,) = kernel_call(corner_kernel, 0, (got1, got0, lines), [(2 * LON_MSG, N)], [(2, *msg), (N, N)])
    near = lax.ppermute(both, "lon", swaps(lons, 0, False))
    plane = (ROWS, N)
    shapes = [(BINS, 1, N, N), (1, N, N), (BINS, N, N)]
    work = [(results(BINS)[1], *plane)] + [(BINS, *plane)] * 4 + [(3, *plane)]
    planes, start, strips, rates, *first_outs = kernel_call(
        own_kernel,
        1,
        (deposition, *large, few, got0, got1, both),
        [(MAIN + EXTRA, *plane), (places(BINS)[1], *plane), (len(STRIPS), *plane), (8, N), *shapes],
        [(2, *msg), *work],
        flops=OWN_FLOPS,
    )
    onward = [(i, (i + (2 if i % 2 == 0 else lons - 2)) % lons) for i in range(lons)]
    near, strips = lax.optimization_barrier((near, strips))
    passed = lax.ppermute(near[LON_MSG:], "lon", onward)
    adj, dens, emis = kernel_call(
        rest_kernel,
        0,
        (planes, start, few, near, *first_outs),
        shapes,
        work,
        aliases={4: 0, 5: 1, 6: 2},
        flops=OWN_FLOPS,
    )
    outs = kernel_call(
        edge_kernel,
        0,
        (rates, strips, near, passed, adj, dens, emis, few),
        shapes,
        [
            (len(STRIPS), *plane),
            (2, LON_MSG, N),
            (len(STRIPS), N, N),
            (places(1)[1], *plane),
            (results(1)[1], *plane),
            (1, *plane),
            (1, *plane),
            (1, *plane),
            (1, *plane),
            (3, *plane),
        ],
        fast=False,
    )
    return tuple(outs)


def solution(mesh):
    return jax.shard_map(
        shards,
        mesh=mesh,
        in_specs=(
            P(None, None, "lat", "lon"),
            P(None, None, "lat", "lon"),
            P(None, "lat", "lon"),
            P(None, "lat", "lon"),
            P(None, "lat", "lon"),
            P(None, "lat", "lon"),
            P(None, "lat", "lon"),
            P("lat", "lon"),
            P("lat", "lon"),
            P(None, "lat", "lon"),
            P(),
        ),
        out_specs=(P(None, None, "lat", "lon"), P(None, "lat", "lon"), P(None, "lat", "lon")),
        check_vma=False,
    )
```
